512 devices in a mesh: gx: 8 (over z), yz: 64 (over x, y, core).
Axes of the slice: x: 4, y: 8, z: 8, core: 2. Of those that a mesh axis runs over, the one named last changes fastest.
Arguments:
- system_source_term: float32 [320, 65536], P(None, ('gx', 'yz')), may hold values from -200 to 200
- mass_plus_source: float32 [320, 65536], P(None, ('gx', 'yz')), may hold values from 1 to 4
- lifted_upwind_coupling: float32 [480, 65536], P(None, ('gx', 'yz')), may hold values from 0.5 to 2
- frozen_direction_derivative: float32 [75, 65536], P(None, ('gx', 'yz')), may hold values from -3 to 3
- first_solve_matrix: float32 [320, 320], replicated, may hold values from -0.3125 to 0.3125
- final_solve_matrix: float32 [320, 320], replicated, may hold values from -0.3125 to 0.3125
- middle_cell_matrices: float32 [320, 65536], P(None, ('gx', 'yz')), may hold values from 0.3 to 3
- adjacent_table_slots: int32 [6, 65536], P(None, ('gx', 'yz')), may hold values from 0 to 1296, as said below
- plane_outgoing_cells: int32 [512, 2, 16], P(('gx', 'yz')), may hold values from 0 to 127
- band_outgoing_cells: int32 [512, 2, 16], P(('gx', 'yz')), may hold values from 0 to 127
- small_side_table_slot: int32 [512, 384], P(('gx', 'yz')), may hold values from 0 to 768, as said below
- proprietor_mortar_index: int32 [512, 384], P(('gx', 'yz')), may hold values from 0 to 80, as said below
- outgoing_quadrant_index: int32 [512, 384], P(('gx', 'yz')), may hold values from 0 to 3, as said below
- incoming_mortar_index: int32 [512, 384], P(('gx', 'yz')), may hold values from 0 to 80
- incoming_quadrant_index: int32 [512, 384], P(('gx', 'yz')), may hold values from 0 to 3, as said below
- coarse_mortar_table_slot: int32 [512, 80], P(('gx', 'yz')), may hold values from 0 to 767
Outputs:
- newton_update: float32 [320, 65536], P(None, ('gx', 'yz'))
The draws below stay inside these ranges and needn't reach their ends.
Inputs may be any that keep to these rules, and one draw needn't show every extreme that they name: `adjacent_table_slots`: column of the neighbour trace in the device's table; 1296 marks a boundary face. `small_side_table_slot`: 768 marks an empty slot, exactly where proprietor_mortar_index is 80. Send slot (m, c) of device (g, k) and receive slot (k, c) of device (g, m) hold the same tile: there proprietor_mortar_index, outgoing_quadrant_index equal incoming_mortar_index, incoming_quadrant_index here; 80 marks an empty slot; no position of an owner's hanging face is sent twice; the live hanging faces of an owner are its first ones; from one device to one owner go at most 6 tiles, a bound reached in every draw; in each gx plane one owner receives 4 * 80 tiles. `outgoing_quadrant_index`: 0 in empty slots. `incoming_quadrant_index`: 0 in empty slots.
All inputs are finite; a program needn't handle non-finite values.
Results may differ from the reference program's by a relative error of at most 0.0003.
Values sent between devices are 32-bit elements; how exact they have to be, the bound alone decides.
A program may use at most 64 MiB of HBM per device.

```python
import math
import jax
import jax.numpy as jnp
import numpy as np
from jax import lax

CELL_DOF_SIZE = 320
FACE = 80
ELEM_DEV = 128
HANG = 80
ITERS = 2
CELL_TOTAL = 65536
HALO_SLOTS = 16
CAP = 6
TABLE = 1296
N_GX = 8
N_YZ = 64


def mortar_lists(key):
    subkeys = jax.random.split(jax.random.fold_in(key, 17), 4)
    period = N_YZ - 1
    slot_count = N_YZ * CAP
    devices = N_GX * N_YZ
    full_shape = (N_GX, N_YZ, 4 * HANG)
    live_count = jax.random.randint(subkeys[0], (N_GX, N_YZ), 1, 3 * HANG // 4 + 1)
    busiest = jax.random.randint(subkeys[1], (N_GX, 1), 0, N_YZ)
    owner_id = jnp.arange(N_YZ, dtype=jnp.int32)[None, :]
    live_count = jnp.where(owner_id == busiest, HANG, live_count)
    offsets = jax.random.randint(subkeys[2], (N_GX, N_YZ), 0, period)
    tile_id = jnp.arange(4 * HANG, dtype=jnp.int32)[None, None, :]
    plane_id = jnp.arange(N_GX, dtype=jnp.int32)[:, None, None]
    owner_three = owner_id[:, :, None]
    source = jnp.broadcast_to((owner_three + 1 + (offsets[:, :, None] + tile_id) % period) % N_YZ, full_shape)
    slot_id = jnp.broadcast_to(tile_id // period, full_shape)
    is_live = tile_id < 4 * live_count[:, :, None]
    hang_value = jnp.broadcast_to(jnp.where(is_live, tile_id // 4, HANG), full_shape).reshape(-1)
    pos_value = jnp.broadcast_to(jnp.where(is_live, tile_id % 4, 0), full_shape).reshape(-1)
    send_row = (plane_id * N_YZ + source).reshape(-1)
    send_col = jnp.broadcast_to(owner_three * CAP + slot_id, full_shape).reshape(-1)
    recv_row = jnp.broadcast_to(plane_id * N_YZ + owner_three, full_shape).reshape(-1)
    recv_col = (source * CAP + slot_id).reshape(-1)
    unused = jnp.full((devices, slot_count), HANG, jnp.int32)
    zeros_int = jnp.zeros((devices, slot_count), jnp.int32)
    proprietor_mortar_index = unused.at[send_row, send_col].set(hang_value)
    outgoing_quadrant_index = zeros_int.at[send_row, send_col].set(pos_value)
    incoming_mortar_index = unused.at[recv_row, recv_col].set(hang_value)
    incoming_quadrant_index = zeros_int.at[recv_row, recv_col].set(pos_value)
    face_pick = jax.random.randint(subkeys[3], (devices, slot_count), 0, 6 * ELEM_DEV)
    small_side_table_slot = jnp.where(proprietor_mortar_index < HANG, face_pick, 6 * ELEM_DEV)
    return (small_side_table_slot, proprietor_mortar_index, outgoing_quadrant_index, incoming_mortar_index, incoming_quadrant_index)


def draw_small_side_table_slot(key, part):
    return mortar_lists(key)[0]


def draw_proprietor_mortar_index(key, part):
    return mortar_lists(key)[1]


def draw_outgoing_quadrant_index(key, part):
    return mortar_lists(key)[2]


def draw_incoming_mortar_index(key, part):
    return mortar_lists(key)[3]


def draw_incoming_quadrant_index(key, part):
    return mortar_lists(key)[4]


def draw_adjacent_table_slots(key, part):
    subkeys = jax.random.split(jax.random.fold_in(key, 3), 5)
    full_shape = (6, CELL_TOTAL)
    category = jax.random.randint(subkeys[0], full_shape, 0, 10)
    face_id = jnp.broadcast_to(jnp.arange(6, dtype=jnp.int32)[:, None], full_shape)
    opposite = face_id + 1 - 2 * (face_id % 2)
    local_column = opposite * ELEM_DEV + jax.random.randint(subkeys[1], full_shape, 0, ELEM_DEV)
    halo_base = 6 * ELEM_DEV + jnp.where(face_id < 2, 0, 2 * HALO_SLOTS) + jnp.where(face_id % 2 == 0, 0, HALO_SLOTS)
    halo_column = halo_base + jax.random.randint(subkeys[2], full_shape, 0, HALO_SLOTS)
    hang_column = 6 * ELEM_DEV + 4 * HALO_SLOTS + jax.random.randint(subkeys[3], full_shape, 0, HANG)
    reply_column = 6 * ELEM_DEV + 4 * HALO_SLOTS + HANG + jax.random.randint(subkeys[4], full_shape, 0, N_YZ * CAP)
    is_halo = (category == 4) | (face_id < 2) & (category == 3)
    chosen = jnp.where(category == 9, TABLE, reply_column)
    chosen = jnp.where(category == 5, hang_column, chosen)
    chosen = jnp.where(category < 5, local_column, chosen)
    chosen = jnp.where(is_halo, halo_column, chosen)
    return chosen.astype(jnp.int32)


def draw_system_source_term(key, part):
    subkeys = jax.random.split(jax.random.fold_in(key, 5), 3)
    columns = jnp.arange(CELL_TOTAL, dtype=jnp.int32)
    device_id = (columns // ELEM_DEV).astype(jnp.float32)
    rising = jnp.exp(jnp.log(3.0) * device_id / (N_GX * N_YZ - 1))
    row_scale = jnp.exp(jax.random.uniform(subkeys[1], (CELL_DOF_SIZE,), jnp.float32, jnp.log(0.3), jnp.log(3.0)))
    column_scale = jnp.exp(jax.random.uniform(subkeys[2], (CELL_TOTAL,), jnp.float32, jnp.log(0.3), jnp.log(3.0)))
    noise = jnp.clip(jax.random.normal(subkeys[0], (CELL_DOF_SIZE, CELL_TOTAL), jnp.float32), -4.0, 4.0)
    return noise * row_scale[:, None] * column_scale[None, :] * rising[None, :]


def plant(values, key, low, largest):
    index_at = [jax.random.randint(jax.random.fold_in(key, axis), (), 0, length) for axis, length in enumerate(values.shape)]
    longest = values.shape.index(max(values.shape))
    beside = index_at[:longest] + [(index_at[longest] + 1) % values.shape[longest]] + index_at[longest + 1:]
    return values.at[tuple(index_at)].set(low).at[tuple(beside)].set(largest)


def block_scale(own_key, dims, cuts, least, top_value):
    level, own = 1.0, jax.random.fold_in(own_key, 6)
    for dim, parts in cuts:
        heights = jnp.exp(jax.random.uniform(jax.random.fold_in(own, dim), (parts,), jnp.float32, least / len(cuts), top_value / len(cuts)))
        level = level * jnp.repeat(heights, dims[dim] // parts).reshape([-1 if axis == dim else 1 for axis in range(len(dims))])
    return level


def scatter_about(own_key, extent, width, limit, cuts=(), held_as=jnp.bfloat16):
    values = width * jax.random.normal(own_key, extent, jnp.float32)
    if cuts:
        values = values * block_scale(own_key, extent, cuts, -0.22, 0.18)
    return jnp.clip(values, -limit, limit).astype(held_as)


def setup_inputs(seed: int = 0) -> dict:
    arg_keys = jax.random.split(jax.random.key(seed), 17)
    return {
        "system_source_term": draw_system_source_term(jax.random.fold_in(arg_keys[16], 71), 0),
        "mass_plus_source": jnp.clip(jnp.exp(math.log(4.0) - 1.3862944 * jax.random.uniform(arg_keys[1], (CELL_DOF_SIZE, CELL_TOTAL), jnp.float32) ** block_scale(arg_keys[1], (CELL_DOF_SIZE, CELL_TOTAL), ((1, 512),), -0.2, 0.2)), 1.0, 4.0),
        "lifted_upwind_coupling": jnp.clip(jnp.exp(math.log(2.0) - 1.3862944 * jax.random.uniform(arg_keys[2], (6 * FACE, CELL_TOTAL), jnp.float32) ** block_scale(arg_keys[2], (6 * FACE, CELL_TOTAL), ((1, 512),), -0.2, 0.2)), 0.5, 2.0),
        "frozen_direction_derivative": scatter_about(arg_keys[3], (75, CELL_TOTAL), 0.5, 3.0, ((1, 512),), jnp.float32),
        "first_solve_matrix": scatter_about(arg_keys[4], (CELL_DOF_SIZE, CELL_DOF_SIZE), CELL_DOF_SIZE ** -0.5, 0.3125, (), jnp.float32),
        "final_solve_matrix": scatter_about(arg_keys[5], (CELL_DOF_SIZE, CELL_DOF_SIZE), CELL_DOF_SIZE ** -0.5, 0.3125, (), jnp.float32),
        "middle_cell_matrices": jnp.clip(jnp.exp(math.log(3.0) - 2.3025851 * jax.random.uniform(arg_keys[6], (CELL_DOF_SIZE, CELL_TOTAL), jnp.float32) ** block_scale(arg_keys[6], (CELL_DOF_SIZE, CELL_TOTAL), ((1, 512),), -0.2, 0.2)), 0.3, 3.0),
        "adjacent_table_slots": draw_adjacent_table_slots(jax.random.fold_in(arg_keys[16], 71), 0),
        "plane_outgoing_cells": plant(jax.random.randint(arg_keys[8], (N_GX * N_YZ, 2, HALO_SLOTS), 0, ELEM_DEV), jax.random.fold_in(arg_keys[8], 1), 0, ELEM_DEV - 1).astype(jnp.int32),
        "band_outgoing_cells": plant(jax.random.randint(arg_keys[9], (N_GX * N_YZ, 2, HALO_SLOTS), 0, ELEM_DEV), jax.random.fold_in(arg_keys[9], 1), 0, ELEM_DEV - 1).astype(jnp.int32),
        "small_side_table_slot": draw_small_side_table_slot(jax.random.fold_in(arg_keys[16], 71), 0),
        "proprietor_mortar_index": draw_proprietor_mortar_index(jax.random.fold_in(arg_keys[16], 71), 0),
        "outgoing_quadrant_index": draw_outgoing_quadrant_index(jax.random.fold_in(arg_keys[16], 71), 0),
        "incoming_mortar_index": draw_incoming_mortar_index(jax.random.fold_in(arg_keys[16], 71), 0),
        "incoming_quadrant_index": draw_incoming_quadrant_index(jax.random.fold_in(arg_keys[16], 71), 0),
        "coarse_mortar_table_slot": plant(jax.random.randint(arg_keys[15], (N_GX * N_YZ, HANG), 0, 6 * ELEM_DEV), jax.random.fold_in(arg_keys[15], 1), 0, (6 * ELEM_DEV) - 1).astype(jnp.int32),
    }


maximum_depth = lax.Precision.HIGHEST
epsilon = 1e-06

def gll_tables():
    inv_root = 1.0 / np.sqrt(5.0)
    gll_points = np.array([-1.0, -inv_root, inv_root, 1.0])
    weights = np.array([1.0, 5.0, 5.0, 1.0]) / 6.0

    def lagrange(points):
        values_at = np.ones((len(points), 4))
        for table_slot_index in range(4):
            for m in range(4):
                if m != table_slot_index:
                    values_at[:, table_slot_index] = values_at[:, table_slot_index] * (points - gll_points[m]) / (gll_points[table_slot_index] - gll_points[m])
        return values_at
    derivative = np.zeros((4, 4))
    for i in range(4):
        for table_slot_index in range(4):
            summed = 0.0
            for m in range(4):
                if m != table_slot_index:
                    product_term = 1.0 / (gll_points[table_slot_index] - gll_points[m])
                    for n in range(4):
                        if n != table_slot_index and n != m:
                            product_term = product_term * (gll_points[i] - gll_points[n]) / (gll_points[table_slot_index] - gll_points[n])
                    summed = summed + product_term
            derivative[i, table_slot_index] = summed
    halves = [lagrange((gll_points - 1.0) / 2.0), lagrange((gll_points + 1.0) / 2.0)]
    half_projections = [0.5 * (1.0 / weights)[:, None] * halve.T * weights[None, :] for halve in halves]
    interpolate = np.stack([np.kron(halves[q // 2], halves[q % 2]) for q in range(4)])
    projection = np.stack([np.kron(half_projections[q // 2], half_projections[q % 2]) for q in range(4)])
    return (jnp.asarray(derivative, jnp.float32), jnp.asarray(interpolate, jnp.float32), jnp.asarray(projection, jnp.float32))

def face_selector(face_id):
    selector = [slice(None)] * 5
    selector[face_id // 2 + 1] = 0 if face_id % 2 == 0 else 3
    return tuple(selector)

def own_traces(argument_array):
    local_count = argument_array.shape[1]
    cube_view = argument_array.reshape(5, 4, 4, 4, local_count)
    return jnp.concatenate([cube_view[face_selector(f)].reshape(80, local_count) for f in range(6)], axis=1)

def jacobian(argument_array, own_faces, near_faces, mass_plus_source, lifted_upwind_coupling, frozen_direction_derivative, derivative):
    local_count = argument_array.shape[1]
    cube_view = argument_array.reshape(5, 4, 4, 4, local_count)
    flux_blocks = frozen_direction_derivative.reshape(3, 5, 5, local_count)
    result = (mass_plus_source * argument_array).reshape(5, 4, 4, 4, local_count)
    contractions = ('mi,aijke->amjke', 'mj,aijke->aimke', 'mk,aijke->aijme')
    for direction in range(3):
        flux_term = jnp.einsum('abe,bijke->aijke', flux_blocks[direction], cube_view, precision=maximum_depth)
        result = result + jnp.einsum(contractions[direction], derivative, flux_term, precision=maximum_depth)
    for face_id in range(6):
        first_col = face_id * local_count
        face_jump = lifted_upwind_coupling[face_id * 80:(face_id + 1) * 80] * (own_faces[:, first_col:first_col + local_count] - near_faces[:, first_col:first_col + local_count])
        result = result.at[face_selector(face_id)].add(face_jump.reshape(5, 4, 4, local_count))
    return result.reshape(320, local_count)

def solve_cell_system(argument_array, first_solve_matrix, final_solve_matrix, middle_cell_matrices):
    interior_share = jnp.dot(first_solve_matrix, argument_array, precision=maximum_depth, preferred_element_type=jnp.float32)
    return jnp.dot(final_solve_matrix, middle_cell_matrices * interior_share, precision=maximum_depth, preferred_element_type=jnp.float32)

def mortar_sums(received, incoming_mortar_index, incoming_quadrant_index, projection, hang_count):
    slot_count = received.shape[1]
    face_values = received.reshape(5, 16, slot_count)
    candidates = jnp.einsum('qmn,anc->qamc', projection, face_values, precision=maximum_depth)
    selector_q = (incoming_quadrant_index[None, :] == jnp.arange(4, dtype=jnp.int32)[:, None]).astype(jnp.float32)
    projected = lax.optimization_barrier(jnp.sum(candidates * selector_q[:, None, None, :], axis=0)).reshape(80, slot_count)
    onehot = (incoming_mortar_index[:, None] == jnp.arange(hang_count, dtype=jnp.int32)[None, :]).astype(jnp.float32)
    return jnp.dot(projected, onehot, precision=maximum_depth, preferred_element_type=jnp.float32)

def fine_replies(coarse_cols, outgoing_quadrant_index, interpolate):
    slot_count = coarse_cols.shape[1]
    face_values = coarse_cols.reshape(5, 16, slot_count)
    candidates = jnp.einsum('qmn,anc->qamc', interpolate, face_values, precision=maximum_depth)
    selector_q = (outgoing_quadrant_index[None, :] == jnp.arange(4, dtype=jnp.int32)[:, None]).astype(jnp.float32)
    return lax.optimization_barrier(jnp.sum(candidates * selector_q[:, None, None, :], axis=0)).reshape(80, slot_count)

def least_squares(beta_norm, columns):
    steps_count = len(columns)
    zero_value = jnp.zeros((), jnp.float32)
    target = [beta_norm] + [zero_value] * steps_count
    rotations = []
    upper_rows = []
    for table_slot_index in range(steps_count):
        column = list(columns[table_slot_index])
        for i in range(len(rotations)):
            cos_value, sine_value = rotations[i]
            first_new = cos_value * column[i] + sine_value * column[i + 1]
            second = cos_value * column[i + 1] - sine_value * column[i]
            column[i] = first_new
            column[i + 1] = second
        radius = jnp.sqrt(column[table_slot_index] * column[table_slot_index] + column[table_slot_index + 1] * column[table_slot_index + 1])
        cos_value = column[table_slot_index] / radius
        sine_value = column[table_slot_index + 1] / radius
        column[table_slot_index] = radius
        rotations.append((cos_value, sine_value))
        target[table_slot_index + 1] = -sine_value * target[table_slot_index]
        target[table_slot_index] = cos_value * target[table_slot_index]
        upper_rows.append(column[:table_slot_index + 1])
    coeffs = [zero_value] * steps_count
    for table_slot_index in reversed(range(steps_count)):
        running = target[table_slot_index]
        for k in range(table_slot_index + 1, steps_count):
            running = running - upper_rows[k][table_slot_index] * coeffs[k]
        coeffs[table_slot_index] = running / upper_rows[table_slot_index][table_slot_index]
    return coeffs

def reference(system_source_term, mass_plus_source, lifted_upwind_coupling, frozen_direction_derivative, first_solve_matrix, final_solve_matrix, middle_cell_matrices, adjacent_table_slots, plane_outgoing_cells, band_outgoing_cells, small_side_table_slot, proprietor_mortar_index, outgoing_quadrant_index, incoming_mortar_index, incoming_quadrant_index, coarse_mortar_table_slot):
    derivative, interpolate, projection = gll_tables()
    devices = N_GX * N_YZ
    slot_count = N_YZ * CAP

    def split_devices(array):
        return array.reshape(array.shape[0], devices, ELEM_DEV).transpose(1, 0, 2)

    def join_devices(array):
        return array.transpose(1, 0, 2).reshape(array.shape[1], devices * ELEM_DEV)
    diag_dev = split_devices(mass_plus_source)
    coef_dev = split_devices(lifted_upwind_coupling)
    flux_dev = split_devices(frozen_direction_derivative)
    near_index = split_devices(adjacent_table_slots).reshape(devices, 6 * ELEM_DEV)

    def pick_pairs(face_table, chosen, first_face):
        return jnp.stack([face_table[:, first_face * ELEM_DEV + chosen[0]], face_table[:, (first_face + 1) * ELEM_DEV + chosen[1]]])

    def take_columns(face_table, column_index):
        return jnp.take(face_table, column_index, axis=1, mode='fill', fill_value=0.0)

    def operator_action(argument_array):
        fields = split_devices(argument_array)
        own_faces = jax.vmap(own_traces)(fields)
        slab_send = jax.vmap(lambda a, b: pick_pairs(a, b, 0))(own_faces, plane_outgoing_cells)
        side_send = jax.vmap(lambda a, b: pick_pairs(a, b, 2))(own_faces, band_outgoing_cells)
        slab_grid = slab_send.reshape(N_GX, N_YZ, 2, 80, HALO_SLOTS)
        side_grid = side_send.reshape(N_GX, N_YZ, 2, 80, HALO_SLOTS)
        blank = jnp.zeros((1, N_YZ, 80, HALO_SLOTS), jnp.float32)
        slab_lower = jnp.concatenate([blank, slab_grid[:-1, :, 1]], axis=0).reshape(devices, 80, HALO_SLOTS)
        slab_upper = jnp.concatenate([slab_grid[1:, :, 0], blank], axis=0).reshape(devices, 80, HALO_SLOTS)
        side_lower = jnp.roll(side_grid[:, :, 1], 1, axis=1).reshape(devices, 80, HALO_SLOTS)
        side_upper = jnp.roll(side_grid[:, :, 0], -1, axis=1).reshape(devices, 80, HALO_SLOTS)
        fine_send = jax.vmap(take_columns)(own_faces, small_side_table_slot)
        fine_recv = fine_send.reshape(N_GX, N_YZ, 80, N_YZ, CAP).transpose(0, 3, 2, 1, 4).reshape(devices, 80, slot_count)
        hang_sum = jax.vmap(lambda a, b, c: mortar_sums(a, b, c, projection, HANG))(fine_recv, incoming_mortar_index, incoming_quadrant_index)
        coarse = jax.vmap(lambda a, b: jnp.take(a, b, axis=1))(own_faces, coarse_mortar_table_slot)
        all_coarse = coarse.reshape(N_GX, N_YZ, 80, HANG).transpose(0, 2, 1, 3).reshape(N_GX, 80, N_YZ * HANG)
        owner_of_slot = jnp.arange(slot_count, dtype=jnp.int32) // CAP
        column_index = jnp.where(proprietor_mortar_index < HANG, owner_of_slot[None, :] * HANG + proprietor_mortar_index, N_YZ * HANG)
        column_index = column_index.reshape(N_GX, N_YZ, slot_count)
        coarse_cols = jax.vmap(lambda a, b: jax.vmap(lambda c: take_columns(a, c))(b))(all_coarse, column_index)
        coarse_cols = coarse_cols.reshape(devices, 80, slot_count)
        replies = jax.vmap(lambda a, b: fine_replies(a, b, interpolate))(coarse_cols, outgoing_quadrant_index)
        trace_table = jnp.concatenate([own_faces, slab_lower, slab_upper, side_lower, side_upper, hang_sum, replies], axis=2)
        near_faces = jax.vmap(take_columns)(trace_table, near_index)
        result = jax.vmap(lambda a, b, c, d, e, f: jacobian(a, b, c, d, e, f, derivative))(fields, own_faces, near_faces, diag_dev, coef_dev, flux_dev)
        return join_devices(result)
    defect_array = solve_cell_system(system_source_term, first_solve_matrix, final_solve_matrix, middle_cell_matrices)
    beta_norm = jnp.sqrt(jnp.sum(defect_array * defect_array) + epsilon)
    arnoldi_directions = [defect_array / beta_norm]
    columns = []
    for table_slot_index in range(ITERS):
        scratch_storage = solve_cell_system(operator_action(arnoldi_directions[table_slot_index]), first_solve_matrix, final_solve_matrix, middle_cell_matrices)
        column = []
        for i in range(table_slot_index + 1):
            coefficient = jnp.sum(scratch_storage * arnoldi_directions[i])
            scratch_storage = scratch_storage - coefficient * arnoldi_directions[i]
            column.append(coefficient)
        new_norm = jnp.sqrt(jnp.sum(scratch_storage * scratch_storage) + epsilon)
        column.append(new_norm)
        columns.append(column)
        arnoldi_directions.append(scratch_storage / new_norm)
    coeffs = least_squares(beta_norm, columns)
    newton_update = coeffs[0] * arnoldi_directions[0]
    for table_slot_index in range(1, ITERS):
        newton_update = newton_update + coeffs[table_slot_index] * arnoldi_directions[table_slot_index]
    return newton_update
```

```python
import functools

import jax
import jax.numpy as jnp
import ml_dtypes
import numpy as np
from jax import lax
from jax.experimental import pallas as pl
from jax.experimental.pallas import tpu as pltpu
from jax.sharding import PartitionSpec as P

MESH = pl.DeviceIdType.MESH
F32 = jnp.float32
BF16 = jnp.bfloat16
I32 = jnp.int32

EPSILON = 1e-6
SCALE = 2.0**-10
CAP = 6
FACE = 80
HALO = 16


def split_np(array):
    high = array.astype(np.float32).astype(ml_dtypes.bfloat16)
    low = (array - high.astype(np.float64)).astype(np.float32).astype(ml_dtypes.bfloat16)
    return high, low


def gll_tables():
    inv_root = 1.0 / np.sqrt(5.0)
    points = np.array([-1.0, -inv_root, inv_root, 1.0])
    weights = np.array([1.0, 5.0, 5.0, 1.0]) / 6.0

    def lagrange(at):
        values = np.ones((len(at), 4))
        for j in range(4):
            for m in range(4):
                if m != j:
                    values[:, j] = values[:, j] * (at - points[m]) / (points[j] - points[m])
        return values

    derivative = np.zeros((4, 4))
    for i in range(4):
        for j in range(4):
            for m in range(4):
                if m != j:
                    term = 1.0 / (points[j] - points[m])
                    for n in range(4):
                        if n != j and n != m:
                            term = term * (points[i] - points[n]) / (points[j] - points[n])
                    derivative[i, j] += term
    halves = [lagrange((points - 1.0) / 2.0), lagrange((points + 1.0) / 2.0)]
    projections = [0.5 * (1.0 / weights)[:, None] * h.T * weights[None, :] for h in halves]
    one5, one4 = np.eye(5), np.eye(4)
    fine = np.concatenate(
        [np.kron(one5, np.kron(projections[q // 2], projections[q % 2])) for q in range(4)], axis=1
    )
    coarse = np.concatenate(
        [np.kron(one5, np.kron(halves[q // 2], halves[q % 2])) for q in range(4)], axis=1
    )
    node = np.concatenate(
        [
            np.kron(derivative, np.kron(one4, one4)),
            np.kron(one4, np.kron(derivative, one4)),
            np.kron(one4, np.kron(one4, derivative)),
        ],
        axis=0,
    )
    select = np.zeros((6, FACE, 320))
    for face in range(6):
        fixed = 3 * (face % 2)
        for a in range(5):
            for p in range(4):
                for q in range(4):
                    n = (
                        fixed * 16 + p * 4 + q,
                        p * 16 + fixed * 4 + q,
                        p * 16 + q * 4 + fixed,
                    )[face // 2]
                    select[face, a * 16 + p * 4 + q, a * 64 + n] = 1.0
    node_high, node_low = split_np(node)
    return (
        np.concatenate([node_high, node_high, node_low], axis=1),
        np.concatenate(split_np(fine), axis=0),
        np.concatenate(split_np(coarse), axis=0),
        select.reshape(480, 320).astype(ml_dtypes.bfloat16),
    )


def split(array):
    high = array.astype(BF16)
    return high, (array - high.astype(F32)).astype(BF16)


def mm(a, b):
    return jnp.dot(a, b, preferred_element_type=F32)


def product(a_high, a_low, b):
    b_high, b_low = split(b)
    n = b.shape[1]
    wide = mm(a_high, jnp.concatenate([b_high, b_low], axis=1))
    return wide[:, :n] + wide[:, n:] + mm(a_low, b_high)


def lanes(shape):
    return lax.broadcasted_iota(I32, shape, 1)


def rows(shape):
    return lax.broadcasted_iota(I32, shape, 0)


def stack_rows(parts, count):
    shape = (count, parts[0].shape[1])
    at = rows(shape)
    out = jnp.zeros(shape, F32)
    for i, part in enumerate(parts):
        out = jnp.where(at == i, part.astype(F32), out)
    return out


def onehot(index, shape):
    return jnp.where(index == rows(shape), 1.0, 0.0).astype(BF16)


def kernel(
    n_gx,
    n_yz,
    hang,
    b_ref,
    mass_ref,
    coef_ref,
    flux_ref,
    first_ref,
    final_ref,
    mid_ref,
    adj_ref,
    plane_ref,
    band_ref,
    small_ref,
    outq_ref,
    incm_ref,
    incq_ref,
    cmts_ref,
    node_ref,
    fine_ref,
    coarse_ref,
    select_ref,
    out_ref,
    x_ref,
    recv_ref,
    hx_ref,
    hrecv_ref,
    gx_ref,
    grecv_ref,
    px_ref,
    precv_ref,
    oh_ref,
    near_own_ref,
    near_in_ref,
    pick_ref,
    lift_ref,
    tr_ref,
    u_ref,
    send_sem,
    recv_sem,
):
    g, k = lax.axis_index("gx"), lax.axis_index("yz")
    wide = 8 * n_yz
    slots = CAP * n_yz
    barrier = pltpu.get_barrier_semaphore()

    def greet(i, _):
        pl.semaphore_signal(
            barrier, inc=1, device_id=(g, lax.rem(k + i, n_yz)), device_id_type=MESH
        )
        return 0

    lax.fori_loop(1, n_yz, greet, 0)
    for i in range(1, n_gx):
        pl.semaphore_signal(
            barrier, inc=1, device_id=(lax.rem(g + i, n_gx), k), device_id_type=MESH
        )

    first_high, first_low = split(first_ref[...])
    final_high, final_low = split(final_ref[...])
    select = select_ref[...]
    pick_ref[0] = mm(select, final_high).astype(BF16)
    pick_ref[1] = mm(select, final_low).astype(BF16)

    mid = mid_ref[...]
    weighted = mid * product(first_high, first_low, b_ref[...])

    lane = lanes((1, wide))
    eighth = jnp.bitwise_and(lane, 7)
    live = eighth < CAP
    small = small_ref[...]
    incm = incm_ref[...]
    parts = [
        jnp.right_shift(small, 5),
        jnp.bitwise_and(small, 31),
        outq_ref[...],
        incm,
        incq_ref[...],
    ]
    target = jnp.where(live, CAP * jnp.right_shift(lane, 3) + eighth, -1)
    spread = mm(stack_rows(parts, 16).astype(BF16), onehot(target, (slots, wide)))
    spread = spread.astype(I32)
    fine_col = jnp.where(live, 32 * spread[0:1] + spread[1:2], -1)
    outq = spread[2:3]
    owned = jnp.where(live & (spread[3:4] < hang), spread[3:4], -1)
    incq = spread[4:5]
    cmts = cmts_ref[...]
    parts = [jnp.right_shift(cmts, 5), jnp.bitwise_and(cmts, 31)]
    found = mm(stack_rows(parts, 16).astype(BF16), onehot(owned, (hang, wide))).astype(I32)
    coarse_col = jnp.where(owned >= 0, 32 * found[0:1] + found[1:2], -1)
    plane, band = plane_ref[0], band_ref[0]
    repeat = jnp.where(
        jnp.bitwise_and(lanes((HALO, 128)), HALO - 1) == rows((HALO, 128)), 1.0, 0.0
    ).astype(BF16)
    halo = mm(
        stack_rows([plane[0:1], plane[1:2], band[0:1], band[1:2]], 16).astype(BF16), repeat
    ).astype(I32)
    group = jnp.right_shift(lanes((1, 128)), 4)
    halo_col = jnp.full((1, 128), -1, I32)
    for i in range(4):
        halo_col = jnp.where(group == i, halo[i : i + 1] + 128 * i, halo_col)
    oh_ref[:, 0:wide] = onehot(fine_col, (768, wide))
    oh_ref[:, wide : 2 * wide] = onehot(coarse_col, (768, wide))
    oh_ref[:, 2 * wide :] = onehot(halo_col, (768, 128))

    node = node_ref[...]
    fine_w, coarse_w = fine_ref[...], coarse_ref[...]

    def project(matrix, high, low, quadrant):
        def spread_out(part):
            return jnp.concatenate(
                [jnp.where(quadrant == q, part, 0.0).astype(BF16) for q in range(4)], axis=0
            )

        both = mm(matrix, spread_out(high))
        return both[:FACE] + both[FACE:] + mm(matrix[:FACE], spread_out(low))

    def send(step, u_traces):
        high, low = split(u_traces)
        tr_ref[0:FACE] = jnp.concatenate(
            [high[FACE * f : FACE * (f + 1)] for f in range(6)], axis=1
        )
        tr_ref[FACE:] = jnp.concatenate([low[FACE * f : FACE * (f + 1)] for f in range(6)], axis=1)
        gathered = mm(tr_ref[...], oh_ref[...])
        halo_out = gathered[:FACE, 2 * wide :] + gathered[FACE:, 2 * wide :]
        halo_out = jnp.concatenate([halo_out, jnp.zeros((48, 128), F32)], axis=0).T
        hx_ref[step] = halo_out[0 : 4 * HALO].reshape(4, HALO, 128)
        fine = project(fine_w, gathered[:FACE, :wide], gathered[FACE:, :wide], outq)
        coarse = project(
            coarse_w,
            gathered[:FACE, wide : 2 * wide],
            gathered[FACE:, wide : 2 * wide],
            incq,
        )
        rest = coarse[48:]
        eight = jnp.bitwise_and(lanes((32, wide)), 7)
        tails = []
        for i in range(4):
            tail = jnp.where(eight == 6, pltpu.roll(rest, 6 - i, 1), 0.0)
            if i < 2:
                tail = jnp.where(eight == 7, pltpu.roll(rest, 3 - i, 1), tail)
            tails.append(tail)
        packed = jnp.where(
            jnp.bitwise_and(lanes((128, wide)), 7) < CAP,
            jnp.concatenate([fine, coarse[:48]], axis=0),
            jnp.concatenate(tails, axis=0),
        )
        x_ref[step] = packed.T.reshape(n_yz, 8, 128)
        if step == 0:
            pl.semaphore_wait(barrier, n_yz + n_gx - 2)
        up_g, down_g = lax.rem(g + 1, n_gx), lax.rem(g + n_gx - 1, n_gx)
        up_k, down_k = lax.rem(k + 1, n_yz), lax.rem(k + n_yz - 1, n_yz)
        for source, target, device in (
            (0, 1, (down_g, k)),
            (1, 0, (up_g, k)),
            (2, 3, (g, down_k)),
            (3, 2, (g, up_k)),
        ):
            pltpu.make_async_remote_copy(
                src_ref=hx_ref.at[step, source],
                dst_ref=hrecv_ref.at[step, target],
                send_sem=send_sem.at[step, 0],
                recv_sem=recv_sem.at[step, 0],
                device_id=device,
                device_id_type=MESH,
            ).start()

        def one(i, _):
            m = lax.rem(k + i, n_yz)
            pltpu.make_async_remote_copy(
                src_ref=x_ref.at[step, m],
                dst_ref=recv_ref.at[step, k],
                send_sem=send_sem.at[step, 1],
                recv_sem=recv_sem.at[step, 1],
                device_id=(g, m),
                device_id_type=MESH,
            ).start()
            return 0

        lax.fori_loop(1, n_yz, one, 0)
        recv_ref[step, pl.ds(k, 1)] = x_ref[step, pl.ds(k, 1)]

    def halo_copy(step):
        return pltpu.make_async_remote_copy(
            src_ref=hx_ref.at[step],
            dst_ref=hrecv_ref.at[step],
            send_sem=send_sem.at[step, 0],
            recv_sem=recv_sem.at[step, 0],
            device_id=(g, k),
            device_id_type=MESH,
        )

    def plane_copy(step):
        return pltpu.make_async_remote_copy(
            src_ref=x_ref.at[step, pl.ds(0, n_yz - 1)],
            dst_ref=recv_ref.at[step, pl.ds(0, n_yz - 1)],
            send_sem=send_sem.at[step, 1],
            recv_sem=recv_sem.at[step, 1],
            device_id=(g, k),
            device_id_type=MESH,
        )

    def receive(step):
        halo_copy(step).wait_recv()
        plane_copy(step).wait_recv()
        tiles = recv_ref[step].reshape(wide, 128).T
        eight = jnp.bitwise_and(lanes((32, wide)), 7)
        rest = jnp.zeros((32, wide), F32)
        for c in range(CAP):
            i, column = c % 4, 6 + c // 4
            moved = pltpu.roll(tiles[32 * i : 32 * i + 32], wide - (column - c), 1)
            rest = jnp.where(eight == c, moved, rest)
        halo_in = hrecv_ref[step].reshape(4 * HALO, 128)
        at = jnp.right_shift(rows((4 * HALO, 128)), 4)
        drop = ((at == 0) & (g == 0)) | ((at == 1) & (g == n_gx - 1))
        halo_in = jnp.where(drop, 0.0, halo_in)
        halo_in = jnp.concatenate([halo_in, jnp.zeros((64, 128), F32)], axis=0).T[:FACE]
        values = jnp.concatenate(
            [tiles[:FACE], jnp.concatenate([tiles[FACE:], rest], axis=0), halo_in], axis=1
        )
        high, low = split(values)
        near = mm(jnp.concatenate([high, low], axis=0), near_in_ref[...])
        return near[:FACE] + near[FACE:]

    def volume(u):
        high, low = split(u)

        def side_by_side(part):
            return jnp.concatenate([part[64 * v : 64 * v + 64] for v in range(5)], axis=1)

        high, low = side_by_side(high), side_by_side(low)
        slopes = mm(node, jnp.concatenate([high, low, high], axis=0))
        out = []
        for a in range(5):
            total = mass_ref[64 * a : 64 * a + 64] * u[64 * a : 64 * a + 64]
            for d in range(3):
                for v in range(5):
                    row = d * 25 + a * 5 + v
                    total = (
                        total
                        + flux_ref[row : row + 1]
                        * slopes[64 * d : 64 * d + 64, 128 * v : 128 * v + 128]
                    )
            out.append(total)
        return product(first_high, first_low, jnp.concatenate(out, axis=0))

    def own_near():
        near = mm(tr_ref[...], near_own_ref[...])
        return near[:FACE] + near[FACE:]

    def finish(base, traces, near_own, near_in):
        near = near_own + near_in
        jumps = jnp.concatenate(
            [
                coef_ref[FACE * f : FACE * (f + 1)]
                * (traces[FACE * f : FACE * (f + 1)] - near[:, 128 * f : 128 * f + 128])
                for f in range(6)
            ],
            axis=0,
        )
        return (mid * SCALE) * (base + product(lift_ref[0], lift_ref[1], jumps))

    def fold(a, b):
        return jnp.sum(a * b, axis=0, keepdims=True)

    traces = product(pick_ref[0], pick_ref[1], weighted)
    send(0, traces)
    u_ref[0] = product(final_high, final_low, weighted)
    nt = (((1,), (1,)), ((), ()))
    lift_ref[0] = lax.dot_general(
        first_high, select, nt, preferred_element_type=F32
    ).astype(BF16)
    lift_ref[1] = lax.dot_general(
        first_low, select, nt, preferred_element_type=F32
    ).astype(BF16)
    table = 768 + 4 * HALO
    owned_col = jnp.broadcast_to(jnp.where(owned >= 0, owned + table, -1), (128, wide)).T
    place = rows((wide, 128))
    reply = jnp.where(
        jnp.bitwise_and(place, 7) < CAP,
        CAP * jnp.right_shift(place, 3) + jnp.bitwise_and(place, 7) + table + hang,
        -1,
    )
    halo_at = rows((128, 128))
    halo_at = jnp.where(halo_at < 4 * HALO, halo_at + 768, -1)
    for f in range(6):
        adj = adj_ref[f : f + 1]
        near_own_ref[:, 128 * f : 128 * f + 128] = onehot(adj, (768, 128))
        near_in_ref[0:wide, 128 * f : 128 * f + 128] = jnp.where(
            owned_col == adj, 1.0, 0.0
        ).astype(BF16)
        near_in_ref[wide : 2 * wide, 128 * f : 128 * f + 128] = jnp.where(
            reply == adj, 1.0, 0.0
        ).astype(BF16)
        near_in_ref[2 * wide :, 128 * f : 128 * f + 128] = jnp.where(
            halo_at == adj, 1.0, 0.0
        ).astype(BF16)
    base = volume(u_ref[0])
    near_own = own_near()
    weighted = finish(base, traces, near_own, receive(0))

    traces = product(pick_ref[0], pick_ref[1], weighted)
    send(1, traces)
    u_ref[1] = product(final_high, final_low, weighted)
    base = volume(u_ref[1])
    near_own = own_near()
    r, u1 = u_ref[0], u_ref[1]
    g00, g01, g11 = fold(r, r), fold(r, u1), fold(u1, u1)
    weighted = finish(base, traces, near_own, receive(1))
    u2 = product(final_high, final_low, weighted)

    mine = stack_rows([g00, g01, g11, fold(r, u2), fold(u1, u2), fold(u2, u2)], 8)
    gx_ref[...] = mine
    for i in range(1, n_gx):
        pltpu.make_async_remote_copy(
            src_ref=gx_ref,
            dst_ref=grecv_ref.at[g],
            send_sem=send_sem.at[2, 0],
            recv_sem=recv_sem.at[2, 0],
            device_id=(lax.rem(g + i, n_gx), k),
            device_id_type=MESH,
        ).start()
    grecv_ref[pl.ds(g, 1)] = mine.reshape(1, 8, 128)
    gram_copy = pltpu.make_async_remote_copy(
        src_ref=grecv_ref.at[pl.ds(0, n_gx - 1)],
        dst_ref=grecv_ref.at[pl.ds(0, n_gx - 1)],
        send_sem=send_sem.at[2, 0],
        recv_sem=recv_sem.at[2, 0],
        device_id=(g, k),
        device_id_type=MESH,
    )
    gram_copy.wait_recv()
    column = jnp.sum(jnp.sum(grecv_ref[...], axis=0), axis=1, keepdims=True)
    diagonal = jnp.where(rows((8, 128)) == lanes((8, 128)), column, 0.0)
    mine = jnp.sum(diagonal, axis=0, keepdims=True)
    px_ref[...] = mine

    def one(i, _):
        pltpu.make_async_remote_copy(
            src_ref=px_ref,
            dst_ref=precv_ref.at[k],
            send_sem=send_sem.at[2, 1],
            recv_sem=recv_sem.at[2, 1],
            device_id=(g, lax.rem(k + i, n_yz)),
            device_id_type=MESH,
        ).start()
        return 0

    lax.fori_loop(1, n_yz, one, 0)
    precv_ref[pl.ds(k, 1)] = mine.reshape(1, 1, 128)
    sum_copy = pltpu.make_async_remote_copy(
        src_ref=precv_ref.at[pl.ds(0, n_yz - 1)],
        dst_ref=precv_ref.at[pl.ds(0, n_yz - 1)],
        send_sem=send_sem.at[2, 1],
        recv_sem=recv_sem.at[2, 1],
        device_id=(g, k),
        device_id_type=MESH,
    )
    sum_copy.wait_recv()
    total = jnp.sum(precv_ref[...], axis=0)
    at = lanes((1, 128))

    def entry(i):
        return jnp.sum(jnp.where(at == i, total, 0.0), axis=1, keepdims=True)

    c_r, c_u = coefficients(*[entry(i) for i in range(6)])
    out_ref[...] = c_r * u_ref[0] + c_u * u_ref[1]

    for step in range(2):
        halo_copy(step).wait_send()
        plane_copy(step).wait_send()
    gram_copy.wait_send()
    sum_copy.wait_send()


def coefficients(g00, g01, g11, g02, g12, g22):
    s = SCALE
    beta = jnp.sqrt(g00 + EPSILON)
    h00 = g01 / (s * beta * beta)
    p1, p0 = 1.0 / s, -h00
    norm = (p1 * p1 * g11 + 2.0 * p1 * p0 * g01 + p0 * p0 * g00) / (beta * beta)
    h10 = jnp.sqrt(jnp.maximum(norm, 0.0) + EPSILON)
    c1, c0 = p1 / (beta * h10), p0 / (beta * h10)
    a2, a1 = c1 / s, c0 / s
    h01 = (a2 * g02 + a1 * g01) / beta
    a0 = -h01 / beta
    h11 = c1 * (a2 * g12 + a1 * g11 + a0 * g01) + c0 * (a2 * g02 + a1 * g01 + a0 * g00)
    a1, a0 = a1 - h11 * c1, a0 - h11 * c0
    norm = a2 * (a2 * g22 + 2.0 * (a1 * g12 + a0 * g02)) + (
        a1 * (a1 * g11 + 2.0 * a0 * g01) + a0 * a0 * g00
    )
    h21 = jnp.sqrt(jnp.maximum(norm, 0.0) + EPSILON)
    radius = jnp.sqrt(h00 * h00 + h10 * h10)
    cos0, sin0 = h00 / radius, h10 / radius
    top = cos0 * h01 + sin0 * h11
    low = cos0 * h11 - sin0 * h01
    length = jnp.sqrt(low * low + h21 * h21)
    y1 = (low / length) * (-sin0 * beta) / length
    y0 = (cos0 * beta - top * y1) / radius
    return y0 / beta + y1 * c0, y1 * c1


def on_device(
    n_gx,
    n_yz,
    source,
    mass,
    coupling,
    flux,
    first,
    final,
    middle,
    adjacent,
    plane,
    band,
    small,
    proprietor,
    outq,
    incm,
    incq,
    cmts,
):
    del proprietor
    tables = [jnp.asarray(t) for t in gll_tables()]
    wide = 8 * n_yz
    arguments = (
        source, mass, coupling, flux, first, final, middle, adjacent, plane, band,
        small, outq, incm, incq, cmts, *tables,
    )
    vmem = pl.BlockSpec(memory_space=pltpu.VMEM)
    return pl.pallas_call(
        functools.partial(kernel, n_gx, n_yz, cmts.shape[1]),
        out_shape=jax.ShapeDtypeStruct(source.shape, F32),
        in_specs=[vmem] * len(arguments),
        out_specs=vmem,
        scratch_shapes=[
            pltpu.VMEM((2, n_yz, 8, 128), F32),
            pltpu.VMEM((2, n_yz, 8, 128), F32),
            pltpu.VMEM((2, 4, HALO, 128), F32),
            pltpu.VMEM((2, 4, HALO, 128), F32),
            pltpu.VMEM((8, 128), F32),
            pltpu.VMEM((n_gx, 8, 128), F32),
            pltpu.VMEM((1, 128), F32),
            pltpu.VMEM((n_yz, 1, 128), F32),
            pltpu.VMEM((768, 2 * wide + 128), BF16),
            pltpu.VMEM((768, 768), BF16),
            pltpu.VMEM((2 * wide + 128, 768), BF16),
            pltpu.VMEM((2, 480, 320), BF16),
            pltpu.VMEM((2, 320, 480), BF16),
            pltpu.VMEM((2 * FACE, 768), BF16),
            pltpu.VMEM((2, 320, 128), F32),
            pltpu.SemaphoreType.DMA((3, 2)),
            pltpu.SemaphoreType.DMA((3, 2)),
        ],
        compiler_params=pltpu.CompilerParams(
            collective_id=0, has_side_effects=True, vmem_limit_bytes=48 * 1024 * 1024
        ),
    )(*arguments)


def solution(mesh):
    n_gx, n_yz = mesh.shape["gx"], mesh.shape["yz"]
    both = ("gx", "yz")
    field, lists = P(None, both), P(both, None)
    return jax.shard_map(
        functools.partial(on_device, n_gx, n_yz),
        mesh=mesh,
        in_specs=(
            field, field, field, field, P(), P(), field, field,
            P(both, None, None), P(both, None, None),
            lists, lists, lists, lists, lists, lists,
        ),
        out_specs=field,
        check_vma=False,
    )
```

```python
import functools

import jax
import jax.numpy as jnp
import ml_dtypes
import numpy as np
from jax import lax
from jax.experimental import pallas as pl
from jax.experimental.pallas import tpu as pltpu
from jax.sharding import PartitionSpec as P

MESH = pl.DeviceIdType.MESH
F32 = jnp.float32
BF16 = jnp.bfloat16
I32 = jnp.int32

EPSILON = 1e-6
SCALE = 2.0**-10
CAP = 6
FACE = 80
HALO = 16


def split_np(array):
    high = array.astype(np.float32).astype(ml_dtypes.bfloat16)
    low = (array - high.astype(np.float64)).astype(np.float32).astype(ml_dtypes.bfloat16)
    return high, low


def gll_tables():
    inv_root = 1.0 / np.sqrt(5.0)
    points = np.array([-1.0, -inv_root, inv_root, 1.0])
    weights = np.array([1.0, 5.0, 5.0, 1.0]) / 6.0

    def lagrange(at):
        values = np.ones((len(at), 4))
        for j in range(4):
            for m in range(4):
                if m != j:
                    values[:, j] = values[:, j] * (at - points[m]) / (points[j] - points[m])
        return values

    derivative = np.zeros((4, 4))
    for i in range(4):
        for j in range(4):
            for m in range(4):
                if m != j:
                    term = 1.0 / (points[j] - points[m])
                    for n in range(4):
                        if n != j and n != m:
                            term = term * (points[i] - points[n]) / (points[j] - points[n])
                    derivative[i, j] += term
    halves = [lagrange((points - 1.0) / 2.0), lagrange((points + 1.0) / 2.0)]
    projections = [0.5 * (1.0 / weights)[:, None] * h.T * weights[None, :] for h in halves]
    one5, one4 = np.eye(5), np.eye(4)
    fine = np.concatenate(
        [np.kron(one5, np.kron(projections[q // 2], projections[q % 2])) for q in range(4)], axis=1
    )
    coarse = np.concatenate(
        [np.kron(one5, np.kron(halves[q // 2], halves[q % 2])) for q in range(4)], axis=1
    )
    node = np.concatenate(
        [
            np.kron(derivative, np.kron(one4, one4)),
            np.kron(one4, np.kron(derivative, one4)),
            np.kron(one4, np.kron(one4, derivative)),
        ],
        axis=0,
    )
    select = np.zeros((6, FACE, 320))
    for face in range(6):
        fixed = 3 * (face % 2)
        for a in range(5):
            for p in range(4):
                for q in range(4):
                    n = (
                        fixed * 16 + p * 4 + q,
                        p * 16 + fixed * 4 + q,
                        p * 16 + q * 4 + fixed,
                    )[face // 2]
                    select[face, a * 16 + p * 4 + q, a * 64 + n] = 1.0
    node_high, node_low = split_np(node)
    return (
        np.concatenate([node_high, node_high, node_low], axis=1),
        np.concatenate(split_np(fine), axis=0),
        np.concatenate(split_np(coarse), axis=0),
        select.reshape(480, 320).astype(ml_dtypes.bfloat16),
    )


def split(array):
    high = array.astype(BF16)
    return high, (array - high.astype(F32)).astype(BF16)


def mm(a, b):
    return jnp.dot(a, b, preferred_element_type=F32)


def product(a_high, a_low, b):
    b_high, b_low = split(b)
    n = b.shape[1]
    wide = mm(a_high, jnp.concatenate([b_high, b_low], axis=1))
    return wide[:, :n] + wide[:, n:] + mm(a_low, b_high)


def lanes(shape):
    return lax.broadcasted_iota(I32, shape, 1)


def rows(shape):
    return lax.broadcasted_iota(I32, shape, 0)


def stack_rows(parts, count):
    shape = (count, parts[0].shape[1])
    at = rows(shape)
    out = jnp.zeros(shape, F32)
    for i, part in enumerate(parts):
        out = jnp.where(at == i, part.astype(F32), out)
    return out


def onehot(index, shape):
    return jnp.where(index == rows(shape), 1.0, 0.0).astype(BF16)


def far_first(size):
    return sorted(range(size), key=lambda d: -min(d, size - d))


def outward(i, size):
    return lax.rem(size // 2 + (i + 1) // 2 * (1 - 2 * lax.rem(i, 2)) + size, size)


def kernel(
    n_gx,
    n_yz,
    hang,
    b_hbm,
    mass_hbm,
    coef_hbm,
    flux_hbm,
    first_hbm,
    final_hbm,
    mid_hbm,
    adj_hbm,
    plane_hbm,
    band_hbm,
    small_hbm,
    outq_hbm,
    incm_hbm,
    incq_hbm,
    cmts_hbm,
    node_hbm,
    fine_hbm,
    coarse_hbm,
    select_hbm,
    out_ref,
    b_ref,
    mass_ref,
    coef_ref,
    flux_ref,
    first_ref,
    final_ref,
    mid_ref,
    adj_ref,
    plane_ref,
    band_ref,
    small_ref,
    outq_ref,
    incm_ref,
    incq_ref,
    cmts_ref,
    node_ref,
    fine_ref,
    coarse_ref,
    select_ref,
    load_sem,
    x_ref,
    recv_ref,
    hx_ref,
    hrecv_ref,
    gx_ref,
    grecv_ref,
    px_ref,
    precv_ref,
    oh_ref,
    near_own_ref,
    near_in_ref,
    pick_ref,
    lift_ref,
    tr_ref,
    u_ref,
    send_sem,
    recv_sem,
):
    g, k = lax.axis_index("gx"), lax.axis_index("yz")
    wide = 8 * n_yz
    slots = CAP * n_yz
    barrier = pltpu.get_barrier_semaphore()

    n_y = 8 if n_yz % 16 == 0 else n_yz // 2
    n_x = n_yz // (2 * n_y)
    x, y, core = k // (2 * n_y), lax.rem(k // 2, n_y), lax.rem(k, 2)

    columns = [
        (lax.rem(x + dx, n_x) * n_y * 2, dx, c)
        for dx in far_first(n_x)
        for c in (1, 0)
    ]
    cores = (core, 1 - core)

    def plane(act):
        def one(i, _):
            at = lax.rem(y + outward(i, n_y), n_y) * 2
            for column, _, c in columns:
                act(column + at + cores[c])
            return 0

        lax.fori_loop(0, n_y - 1, one, 0)
        for column, dx, c in columns:
            if dx or c:
                act(column + y * 2 + cores[c])

    def greet(device):
        pl.semaphore_signal(barrier, inc=1, device_id=(g, device), device_id_type=MESH)

    plane(greet)
    gx_partners = [lax.rem(g + dg, n_gx) for dg in far_first(n_gx) if dg]
    for partner_g in gx_partners:
        pl.semaphore_signal(barrier, inc=1, device_id=(partner_g, k), device_id_type=MESH)
    loads = {}
    for i, (name, source, target) in enumerate(
        (
            ("first", first_hbm, first_ref),
            ("b", b_hbm, b_ref),
            ("small", small_hbm, small_ref),
            ("outq", outq_hbm, outq_ref),
            ("incm", incm_hbm, incm_ref),
            ("incq", incq_hbm, incq_ref),
            ("cmts", cmts_hbm, cmts_ref),
            ("plane", plane_hbm, plane_ref),
            ("band", band_hbm, band_ref),
            ("mid", mid_hbm, mid_ref),
            ("final", final_hbm, final_ref),
            ("select", select_hbm, select_ref),
            ("fine", fine_hbm, fine_ref),
            ("coarse", coarse_hbm, coarse_ref),
            ("node", node_hbm, node_ref),
            ("mass", mass_hbm, mass_ref),
            ("flux", flux_hbm, flux_ref),
            ("coef", coef_hbm, coef_ref),
            ("adj", adj_hbm, adj_ref),
        )
    ):
        loads[name] = pltpu.make_async_copy(source, target, load_sem.at[i])
        loads[name].start()

    def ready(*wanted):
        for name in wanted:
            loads[name].wait()

    ready("first", "b", "small", "outq", "incm", "incq", "cmts", "plane", "band")
    ready("mid", "final", "select", "fine", "coarse")
    first_high, first_low = split(first_ref[...])
    final_high, final_low = split(final_ref[...])
    select = select_ref[...]
    pick_ref[0] = mm(select, final_high).astype(BF16)
    pick_ref[1] = mm(select, final_low).astype(BF16)

    mid = mid_ref[...]
    weighted = mid * product(first_high, first_low, b_ref[...])

    lane = lanes((1, wide))
    eighth = jnp.bitwise_and(lane, 7)
    live = eighth < CAP
    small = small_ref[...]
    incm = incm_ref[...]
    parts = [
        jnp.right_shift(small, 5),
        jnp.bitwise_and(small, 31),
        outq_ref[...],
        incm,
        incq_ref[...],
    ]
    target = jnp.where(live, CAP * jnp.right_shift(lane, 3) + eighth, -1)
    spread = mm(stack_rows(parts, 16).astype(BF16), onehot(target, (slots, wide)))
    spread = spread.astype(I32)
    fine_col = jnp.where(live, 32 * spread[0:1] + spread[1:2], -1)
    outq = spread[2:3]
    owned = jnp.where(live & (spread[3:4] < hang), spread[3:4], -1)
    incq = spread[4:5]
    cmts = cmts_ref[...]
    parts = [jnp.right_shift(cmts, 5), jnp.bitwise_and(cmts, 31)]
    found = mm(stack_rows(parts, 16).astype(BF16), onehot(owned, (hang, wide))).astype(I32)
    coarse_col = jnp.where(owned >= 0, 32 * found[0:1] + found[1:2], -1)
    slab, side = plane_ref[0], band_ref[0]
    repeat = jnp.where(
        jnp.bitwise_and(lanes((HALO, 128)), HALO - 1) == rows((HALO, 128)), 1.0, 0.0
    ).astype(BF16)
    halo = mm(
        stack_rows([slab[0:1], slab[1:2], side[0:1], side[1:2]], 16).astype(BF16), repeat
    ).astype(I32)
    group = jnp.right_shift(lanes((1, 128)), 4)
    halo_col = jnp.full((1, 128), -1, I32)
    for i in range(4):
        halo_col = jnp.where(group == i, halo[i : i + 1] + 128 * i, halo_col)
    oh_ref[:, 0:wide] = onehot(fine_col, (768, wide))
    oh_ref[:, wide : 2 * wide] = onehot(coarse_col, (768, wide))
    oh_ref[:, 2 * wide :] = onehot(halo_col, (768, 128))

    fine_w, coarse_w = fine_ref[...], coarse_ref[...]

    def masks(quadrant):
        return [jnp.where(quadrant == q, 1.0, 0.0).astype(BF16) for q in range(4)]

    out_masks, in_masks = masks(outq), masks(incq)

    def project(matrix, high, low, mask):
        def spread_out(part):
            part = part.astype(BF16)
            return jnp.concatenate([part * mask[q] for q in range(4)], axis=0)

        both = mm(matrix, spread_out(high))
        return both[:FACE] + both[FACE:] + mm(matrix[:FACE], spread_out(low))

    def send(step, u_traces):
        high, low = split(u_traces)
        tr_ref[0:FACE] = jnp.concatenate(
            [high[FACE * f : FACE * (f + 1)] for f in range(6)], axis=1
        )
        tr_ref[FACE:] = jnp.concatenate([low[FACE * f : FACE * (f + 1)] for f in range(6)], axis=1)
        gathered = mm(tr_ref[...], oh_ref[...])
        halo_out = gathered[:FACE, 2 * wide :] + gathered[FACE:, 2 * wide :]
        halo_out = jnp.concatenate([halo_out, jnp.zeros((48, 128), F32)], axis=0).T
        hx_ref[step] = halo_out[0 : 4 * HALO].reshape(4, HALO, 128)
        fine = project(fine_w, gathered[:FACE, :wide], gathered[FACE:, :wide], out_masks)
        coarse = project(
            coarse_w,
            gathered[:FACE, wide : 2 * wide],
            gathered[FACE:, wide : 2 * wide],
            in_masks,
        )
        rest = coarse[48:]
        eight = jnp.bitwise_and(lanes((32, wide)), 7)
        tails = []
        for i in range(4):
            tail = jnp.where(eight == 6, pltpu.roll(rest, 6 - i, 1), 0.0)
            if i < 2:
                tail = jnp.where(eight == 7, pltpu.roll(rest, 3 - i, 1), tail)
            tails.append(tail)
        packed = jnp.where(
            jnp.bitwise_and(lanes((128, wide)), 7) < CAP,
            jnp.concatenate([fine, coarse[:48]], axis=0),
            jnp.concatenate(tails, axis=0),
        )
        x_ref[step] = packed.T.reshape(n_yz, 8, 128)
        if step == 0:
            pl.semaphore_wait(barrier, n_yz + n_gx - 2)
        def one(m):
            pltpu.make_async_remote_copy(
                src_ref=x_ref.at[step, m],
                dst_ref=recv_ref.at[step, k],
                send_sem=send_sem.at[step, 1],
                recv_sem=recv_sem.at[step, 1],
                device_id=(g, m),
                device_id_type=MESH,
            ).start()

        plane(one)
        up_g, down_g = lax.rem(g + 1, n_gx), lax.rem(g + n_gx - 1, n_gx)
        up_k, down_k = lax.rem(k + 1, n_yz), lax.rem(k + n_yz - 1, n_yz)
        for source, target, device in (
            (0, 1, (down_g, k)),
            (1, 0, (up_g, k)),
            (2, 3, (g, down_k)),
            (3, 2, (g, up_k)),
        ):
            pltpu.make_async_remote_copy(
                src_ref=hx_ref.at[step, source],
                dst_ref=hrecv_ref.at[step, target],
                send_sem=send_sem.at[step, 0],
                recv_sem=recv_sem.at[step, 0],
                device_id=device,
                device_id_type=MESH,
            ).start()
        recv_ref[step, pl.ds(k, 1)] = x_ref[step, pl.ds(k, 1)]

    def halo_copy(step):
        return pltpu.make_async_remote_copy(
            src_ref=hx_ref.at[step],
            dst_ref=hrecv_ref.at[step],
            send_sem=send_sem.at[step, 0],
            recv_sem=recv_sem.at[step, 0],
            device_id=(g, k),
            device_id_type=MESH,
        )

    def plane_copy(step):
        return pltpu.make_async_remote_copy(
            src_ref=x_ref.at[step, pl.ds(0, n_yz - 1)],
            dst_ref=recv_ref.at[step, pl.ds(0, n_yz - 1)],
            send_sem=send_sem.at[step, 1],
            recv_sem=recv_sem.at[step, 1],
            device_id=(g, k),
            device_id_type=MESH,
        )

    def receive(step):
        halo_copy(step).wait_recv()
        plane_copy(step).wait_recv()
        tiles = recv_ref[step].reshape(wide, 128).T
        eight = jnp.bitwise_and(lanes((32, wide)), 7)
        rest = jnp.zeros((32, wide), F32)
        for c in range(CAP):
            i, column = c % 4, 6 + c // 4
            moved = pltpu.roll(tiles[32 * i : 32 * i + 32], wide - (column - c), 1)
            rest = jnp.where(eight == c, moved, rest)
        halo_in = hrecv_ref[step].reshape(4 * HALO, 128)
        at = jnp.right_shift(rows((4 * HALO, 128)), 4)
        drop = ((at == 0) & (g == 0)) | ((at == 1) & (g == n_gx - 1))
        halo_in = jnp.where(drop, 0.0, halo_in)
        halo_in = jnp.concatenate([halo_in, jnp.zeros((64, 128), F32)], axis=0).T[:FACE]
        values = jnp.concatenate(
            [tiles[:FACE], jnp.concatenate([tiles[FACE:], rest], axis=0), halo_in], axis=1
        )
        high, low = split(values)
        near = mm(jnp.concatenate([high, low], axis=0), near_in_ref[...])
        return near[:FACE] + near[FACE:]

    def volume(u):
        high, low = split(u)
        node = node_ref[...]

        def side_by_side(part):
            return jnp.concatenate([part[64 * v : 64 * v + 64] for v in range(5)], axis=1)

        high, low = side_by_side(high), side_by_side(low)
        slopes = mm(node, jnp.concatenate([high, low, high], axis=0))
        out = []
        for a in range(5):
            total = mass_ref[64 * a : 64 * a + 64] * u[64 * a : 64 * a + 64]
            for d in range(3):
                for v in range(5):
                    row = d * 25 + a * 5 + v
                    total = (
                        total
                        + flux_ref[row : row + 1]
                        * slopes[64 * d : 64 * d + 64, 128 * v : 128 * v + 128]
                    )
            out.append(total)
        return product(first_high, first_low, jnp.concatenate(out, axis=0))

    def own_near():
        near = mm(tr_ref[...], near_own_ref[...])
        return near[:FACE] + near[FACE:]

    def finish(base, traces, near_own, near_in):
        near = near_own + near_in
        jumps = jnp.concatenate(
            [
                coef_ref[FACE * f : FACE * (f + 1)]
                * (traces[FACE * f : FACE * (f + 1)] - near[:, 128 * f : 128 * f + 128])
                for f in range(6)
            ],
            axis=0,
        )
        return (mid * SCALE) * (base + product(lift_ref[0], lift_ref[1], jumps))

    def fold(a, b):
        return jnp.sum(a * b, axis=0, keepdims=True)

    traces = product(pick_ref[0], pick_ref[1], weighted)
    send(0, traces)
    u_ref[0] = product(final_high, final_low, weighted)
    nt = (((1,), (1,)), ((), ()))
    lift_ref[0] = lax.dot_general(
        first_high, select, nt, preferred_element_type=F32
    ).astype(BF16)
    lift_ref[1] = lax.dot_general(
        first_low, select, nt, preferred_element_type=F32
    ).astype(BF16)
    ready("node", "mass", "flux", "coef", "adj")
    table = 768 + 4 * HALO
    owned_col = jnp.broadcast_to(jnp.where(owned >= 0, owned + table, -1), (128, wide)).T
    place = rows((wide, 128))
    reply = jnp.where(
        jnp.bitwise_and(place, 7) < CAP,
        CAP * jnp.right_shift(place, 3) + jnp.bitwise_and(place, 7) + table + hang,
        -1,
    )
    halo_at = rows((128, 128))
    halo_at = jnp.where(halo_at < 4 * HALO, halo_at + 768, -1)
    for f in range(6):
        adj = adj_ref[f : f + 1]
        near_own_ref[:, 128 * f : 128 * f + 128] = onehot(adj, (768, 128))
        near_in_ref[0:wide, 128 * f : 128 * f + 128] = jnp.where(
            owned_col == adj, 1.0, 0.0
        ).astype(BF16)
        near_in_ref[wide : 2 * wide, 128 * f : 128 * f + 128] = jnp.where(
            reply == adj, 1.0, 0.0
        ).astype(BF16)
        near_in_ref[2 * wide :, 128 * f : 128 * f + 128] = jnp.where(
            halo_at == adj, 1.0, 0.0
        ).astype(BF16)
    base = volume(u_ref[0])
    near_own = own_near()
    weighted = finish(base, traces, near_own, receive(0))

    traces = product(pick_ref[0], pick_ref[1], weighted)
    send(1, traces)
    u_ref[1] = product(final_high, final_low, weighted)
    base = volume(u_ref[1])
    near_own = own_near()
    r, u1 = u_ref[0], u_ref[1]
    g00, g01, g11 = fold(r, r), fold(r, u1), fold(u1, u1)
    weighted = finish(base, traces, near_own, receive(1))
    u2 = product(final_high, final_low, weighted)

    mine = stack_rows([g00, g01, g11, fold(r, u2), fold(u1, u2), fold(u2, u2)], 8)
    gx_ref[...] = mine
    for partner_g in gx_partners:
        pltpu.make_async_remote_copy(
            src_ref=gx_ref,
            dst_ref=grecv_ref.at[g],
            send_sem=send_sem.at[2, 0],
            recv_sem=recv_sem.at[2, 0],
            device_id=(partner_g, k),
            device_id_type=MESH,
        ).start()
    grecv_ref[pl.ds(g, 1)] = mine.reshape(1, 8, 128)
    gram_copy = pltpu.make_async_remote_copy(
        src_ref=grecv_ref.at[pl.ds(0, n_gx - 1)],
        dst_ref=grecv_ref.at[pl.ds(0, n_gx - 1)],
        send_sem=send_sem.at[2, 0],
        recv_sem=recv_sem.at[2, 0],
        device_id=(g, k),
        device_id_type=MESH,
    )
    gram_copy.wait_recv()
    column = jnp.sum(jnp.sum(grecv_ref[...], axis=0), axis=1, keepdims=True)
    diagonal = jnp.where(rows((8, 128)) == lanes((8, 128)), column, 0.0)
    mine = jnp.sum(diagonal, axis=0, keepdims=True)
    px_ref[...] = mine

    def one(m):
        pltpu.make_async_remote_copy(
            src_ref=px_ref,
            dst_ref=precv_ref.at[k],
            send_sem=send_sem.at[2, 1],
            recv_sem=recv_sem.at[2, 1],
            device_id=(g, m),
            device_id_type=MESH,
        ).start()

    plane(one)
    precv_ref[pl.ds(k, 1)] = mine.reshape(1, 1, 128)
    sum_copy = pltpu.make_async_remote_copy(
        src_ref=precv_ref.at[pl.ds(0, n_yz - 1)],
        dst_ref=precv_ref.at[pl.ds(0, n_yz - 1)],
        send_sem=send_sem.at[2, 1],
        recv_sem=recv_sem.at[2, 1],
        device_id=(g, k),
        device_id_type=MESH,
    )
    sum_copy.wait_recv()
    total = jnp.sum(precv_ref[...], axis=0)
    at = lanes((1, 128))

    def entry(i):
        return jnp.sum(jnp.where(at == i, total, 0.0), axis=1, keepdims=True)

    c_r, c_u = coefficients(*[entry(i) for i in range(6)])
    out_ref[...] = c_r * u_ref[0] + c_u * u_ref[1]

    for step in range(2):
        halo_copy(step).wait_send()
        plane_copy(step).wait_send()
    gram_copy.wait_send()
    sum_copy.wait_send()


def coefficients(g00, g01, g11, g02, g12, g22):
    s = SCALE
    beta = jnp.sqrt(g00 + EPSILON)
    h00 = g01 / (s * beta * beta)
    p1, p0 = 1.0 / s, -h00
    norm = (p1 * p1 * g11 + 2.0 * p1 * p0 * g01 + p0 * p0 * g00) / (beta * beta)
    h10 = jnp.sqrt(jnp.maximum(norm, 0.0) + EPSILON)
    c1, c0 = p1 / (beta * h10), p0 / (beta * h10)
    a2, a1 = c1 / s, c0 / s
    h01 = (a2 * g02 + a1 * g01) / beta
    a0 = -h01 / beta
    h11 = c1 * (a2 * g12 + a1 * g11 + a0 * g01) + c0 * (a2 * g02 + a1 * g01 + a0 * g00)
    a1, a0 = a1 - h11 * c1, a0 - h11 * c0
    norm = a2 * (a2 * g22 + 2.0 * (a1 * g12 + a0 * g02)) + (
        a1 * (a1 * g11 + 2.0 * a0 * g01) + a0 * a0 * g00
    )
    h21 = jnp.sqrt(jnp.maximum(norm, 0.0) + EPSILON)
    radius = jnp.sqrt(h00 * h00 + h10 * h10)
    cos0, sin0 = h00 / radius, h10 / radius
    top = cos0 * h01 + sin0 * h11
    low = cos0 * h11 - sin0 * h01
    length = jnp.sqrt(low * low + h21 * h21)
    y1 = (low / length) * (-sin0 * beta) / length
    y0 = (cos0 * beta - top * y1) / radius
    return y0 / beta + y1 * c0, y1 * c1


def on_device(
    n_gx,
    n_yz,
    source,
    mass,
    coupling,
    flux,
    first,
    final,
    middle,
    adjacent,
    plane,
    band,
    small,
    proprietor,
    outq,
    incm,
    incq,
    cmts,
):
    del proprietor
    tables = [jnp.asarray(t) for t in gll_tables()]
    wide = 8 * n_yz
    arguments = (
        source, mass, coupling, flux, first, final, middle, adjacent, plane, band,
        small, outq, incm, incq, cmts, *tables,
    )
    vmem = pl.BlockSpec(memory_space=pltpu.VMEM)
    hbm = pl.BlockSpec(memory_space=pltpu.HBM)
    return pl.pallas_call(
        functools.partial(kernel, n_gx, n_yz, cmts.shape[1]),
        out_shape=jax.ShapeDtypeStruct(source.shape, F32),
        in_specs=[hbm] * len(arguments),
        out_specs=vmem,
        scratch_shapes=[
            *[pltpu.VMEM(a.shape, a.dtype) for a in arguments],
            pltpu.SemaphoreType.DMA((len(arguments),)),
            pltpu.VMEM((2, n_yz, 8, 128), F32),
            pltpu.VMEM((2, n_yz, 8, 128), F32),
            pltpu.VMEM((2, 4, HALO, 128), F32),
            pltpu.VMEM((2, 4, HALO, 128), F32),
            pltpu.VMEM((8, 128), F32),
            pltpu.VMEM((n_gx, 8, 128), F32),
            pltpu.VMEM((1, 128), F32),
            pltpu.VMEM((n_yz, 1, 128), F32),
            pltpu.VMEM((768, 2 * wide + 128), BF16),
            pltpu.VMEM((768, 768), BF16),
            pltpu.VMEM((2 * wide + 128, 768), BF16),
            pltpu.VMEM((2, 480, 320), BF16),
            pltpu.VMEM((2, 320, 480), BF16),
            pltpu.VMEM((2 * FACE, 768), BF16),
            pltpu.VMEM((2, 320, 128), F32),
            pltpu.SemaphoreType.DMA((3, 2)),
            pltpu.SemaphoreType.DMA((3, 2)),
        ],
        compiler_params=pltpu.CompilerParams(
            collective_id=0, has_side_effects=True, vmem_limit_bytes=63 * 1024 * 1024
        ),
    )(*arguments)


def solution(mesh):
    n_gx, n_yz = mesh.shape["gx"], mesh.shape["yz"]
    both = ("gx", "yz")
    field, lists = P(None, both), P(both, None)
    return jax.shard_map(
        functools.partial(on_device, n_gx, n_yz),
        mesh=mesh,
        in_specs=(
            field, field, field, field, P(), P(), field, field,
            P(both, None, None), P(both, None, None),
            lists, lists, lists, lists, lists, lists,
        ),
        out_specs=field,
        check_vma=False,
    )
```

```python
import functools

import jax
import jax.numpy as jnp
import ml_dtypes
import numpy as np
from jax import lax
from jax.experimental import pallas as pl
from jax.experimental.pallas import tpu as pltpu
from jax.sharding import PartitionSpec as P

MESH = pl.DeviceIdType.MESH
F32 = jnp.float32
BF16 = jnp.bfloat16
I32 = jnp.int32

EPSILON = 1e-6
SCALE = 2.0**-10
CAP = 6
FACE = 80
HALO = 16
HEAD = 128 - FACE


def split_np(array):
    high = array.astype(np.float32).astype(ml_dtypes.bfloat16)
    low = (array - high.astype(np.float64)).astype(np.float32).astype(ml_dtypes.bfloat16)
    return high, low


def gll_tables():
    inv_root = 1.0 / np.sqrt(5.0)
    points = np.array([-1.0, -inv_root, inv_root, 1.0])
    weights = np.array([1.0, 5.0, 5.0, 1.0]) / 6.0

    def lagrange(at):
        values = np.ones((len(at), 4))
        for j in range(4):
            for m in range(4):
                if m != j:
                    values[:, j] = values[:, j] * (at - points[m]) / (points[j] - points[m])
        return values

    derivative = np.zeros((4, 4))
    for i in range(4):
        for j in range(4):
            for m in range(4):
                if m != j:
                    term = 1.0 / (points[j] - points[m])
                    for n in range(4):
                        if n != j and n != m:
                            term = term * (points[i] - points[n]) / (points[j] - points[n])
                    derivative[i, j] += term
    halves = [lagrange((points - 1.0) / 2.0), lagrange((points + 1.0) / 2.0)]
    projections = [0.5 * (1.0 / weights)[:, None] * h.T * weights[None, :] for h in halves]
    one5, one4 = np.eye(5), np.eye(4)
    fine = np.concatenate(
        [np.kron(one5, np.kron(projections[q // 2], projections[q % 2])) for q in range(4)], axis=1
    )
    coarse = np.concatenate(
        [np.kron(one5, np.kron(halves[q // 2], halves[q % 2])) for q in range(4)], axis=1
    )
    node = np.concatenate(
        [
            np.kron(derivative, np.kron(one4, one4)),
            np.kron(one4, np.kron(derivative, one4)),
            np.kron(one4, np.kron(one4, derivative)),
        ],
        axis=0,
    )
    select = np.zeros((6, FACE, 320))
    for face in range(6):
        fixed = 3 * (face % 2)
        for a in range(5):
            for p in range(4):
                for q in range(4):
                    n = (
                        fixed * 16 + p * 4 + q,
                        p * 16 + fixed * 4 + q,
                        p * 16 + q * 4 + fixed,
                    )[face // 2]
                    select[face, a * 16 + p * 4 + q, a * 64 + n] = 1.0
    node_high, node_low = split_np(node)
    return (
        np.concatenate([node_high, node_high, node_low], axis=1),
        np.concatenate(split_np(fine), axis=0),
        np.concatenate(split_np(coarse), axis=0),
        select.reshape(480, 320).astype(ml_dtypes.bfloat16),
    )


def split(array):
    high = array.astype(BF16)
    return high, (array - high.astype(F32)).astype(BF16)


def mm(a, b):
    return jnp.dot(a, b, preferred_element_type=F32)


def side_by_side(high, low):
    return jnp.concatenate([high[:, :256], low[:, :256], high[:, 256:], low[:, 256:]], axis=1)


def product(a, b):
    high, low = split(b)
    blank = jnp.zeros_like(low)
    both = mm(
        a,
        jnp.concatenate(
            [
                jnp.concatenate([high[:256], high[:256], high[256:], high[256:]], axis=0),
                jnp.concatenate([low[:256], blank[:256], low[256:], blank[256:]], axis=0),
            ],
            axis=1,
        ),
    )
    n = b.shape[1]
    return both[:, :n] + both[:, n:]


def lanes(shape):
    return lax.broadcasted_iota(I32, shape, 1)


def rows(shape):
    return lax.broadcasted_iota(I32, shape, 0)


def stack_rows(parts, count):
    shape = (count, parts[0].shape[1])
    at = rows(shape)
    out = jnp.zeros(shape, F32)
    for i, part in enumerate(parts):
        out = jnp.where(at == i, part.astype(F32), out)
    return out


def onehot(index, shape):
    return jnp.where(index == rows(shape), 1.0, 0.0).astype(BF16)


def far_first(size):
    return sorted(range(size), key=lambda d: -min(d, size - d))


def outward(i, size):
    return lax.rem(size // 2 + (i + 1) // 2 * (1 - 2 * lax.rem(i, 2)) + size, size)


def kernel(
    n_gx,
    n_yz,
    hang,
    b_hbm,
    mass_hbm,
    coef_hbm,
    flux_hbm,
    first_hbm,
    final_hbm,
    mid_hbm,
    adj_hbm,
    plane_hbm,
    band_hbm,
    small_hbm,
    outq_hbm,
    incm_hbm,
    incq_hbm,
    cmts_hbm,
    node_hbm,
    fine_hbm,
    coarse_hbm,
    select_hbm,
    out_ref,
    b_ref,
    mass_ref,
    coef_ref,
    flux_ref,
    first_ref,
    final_ref,
    mid_ref,
    adj_ref,
    plane_ref,
    band_ref,
    small_ref,
    outq_ref,
    incm_ref,
    incq_ref,
    cmts_ref,
    node_ref,
    fine_ref,
    coarse_ref,
    select_ref,
    load_sem,
    x_ref,
    recv_ref,
    hx_ref,
    hrecv_ref,
    gx_ref,
    grecv_ref,
    px_ref,
    precv_ref,
    oh_ref,
    near_own_ref,
    near_in_ref,
    pick_ref,
    lift_ref,
    tr_ref,
    u_ref,
    send_sem,
    recv_sem,
):
    g, k = lax.axis_index("gx"), lax.axis_index("yz")
    wide = 8 * n_yz
    slots = CAP * n_yz
    half = n_yz
    barrier = pltpu.get_barrier_semaphore()

    n_y = 8 if n_yz % 16 == 0 else n_yz // 2
    n_x = n_yz // (2 * n_y)
    x, y, core = k // (2 * n_y), lax.rem(k // 2, n_y), lax.rem(k, 2)

    columns = [
        (lax.rem(x + dx, n_x) * n_y * 2, dx, c)
        for dx in far_first(n_x)
        for c in (1, 0)
    ]
    cores = (core, 1 - core)

    def plane(act):
        def one(i, _):
            at = lax.rem(y + outward(i, n_y), n_y) * 2
            for column, _, c in columns:
                act(column + at + cores[c])
            return 0

        lax.fori_loop(0, n_y - 1, one, 0)
        for column, dx, c in columns:
            if dx or c:
                act(column + y * 2 + cores[c])

    mine = pl.ds(pl.multiple_of(8 * k, 8), 8)

    def greet(device):
        pl.semaphore_signal(barrier, inc=1, device_id=(g, device), device_id_type=MESH)

    plane(greet)
    gx_partners = [lax.rem(g + dg, n_gx) for dg in far_first(n_gx) if dg]
    for partner_g in gx_partners:
        pl.semaphore_signal(barrier, inc=1, device_id=(partner_g, k), device_id_type=MESH)
    loads = {}
    for i, (name, source, target) in enumerate(
        (
            ("first", first_hbm, first_ref),
            ("b", b_hbm, b_ref),
            ("small", small_hbm, small_ref),
            ("outq", outq_hbm, outq_ref),
            ("incm", incm_hbm, incm_ref),
            ("incq", incq_hbm, incq_ref),
            ("cmts", cmts_hbm, cmts_ref),
            ("plane", plane_hbm, plane_ref),
            ("band", band_hbm, band_ref),
            ("mid", mid_hbm, mid_ref),
            ("final", final_hbm, final_ref),
            ("select", select_hbm, select_ref),
            ("fine", fine_hbm, fine_ref),
            ("coarse", coarse_hbm, coarse_ref),
            ("node", node_hbm, node_ref),
            ("mass", mass_hbm, mass_ref),
            ("flux", flux_hbm, flux_ref),
            ("coef", coef_hbm, coef_ref),
            ("adj", adj_hbm, adj_ref),
        )
    ):
        loads[name] = pltpu.make_async_copy(source, target, load_sem.at[i])
        loads[name].start()

    def ready(*wanted):
        for name in wanted:
            loads[name].wait()

    ready("first", "b", "small", "outq", "incm", "incq", "cmts", "plane", "band")
    ready("mid", "final", "select", "fine", "coarse")
    first_high, first_low = split(first_ref[...])
    final_high, final_low = split(final_ref[...])
    first = side_by_side(first_high, first_low)
    final = side_by_side(final_high, final_low)
    select = select_ref[...]
    pick_ref[...] = mm(select, final).astype(BF16)

    mid = mid_ref[...]
    weighted = mid * product(first, b_ref[...])

    lane = lanes((1, slots))
    small = small_ref[...]
    incm = incm_ref[...]
    parts = [
        jnp.right_shift(small, 5),
        jnp.bitwise_and(small, 31),
        outq_ref[...],
        incm,
        incq_ref[...],
    ]
    natural = CAP * lax.rem(lane, n_yz) + lane // n_yz
    spread = mm(stack_rows(parts, 16).astype(BF16), onehot(natural, (slots, slots)))
    spread = spread.astype(I32)
    fine_col = 32 * spread[0:1] + spread[1:2]
    outq = spread[2:3]
    owned = jnp.where(spread[3:4] < hang, spread[3:4], -1)
    incq = spread[4:5]
    cmts = cmts_ref[...]
    parts = [jnp.right_shift(cmts, 5), jnp.bitwise_and(cmts, 31)]
    found = mm(stack_rows(parts, 16).astype(BF16), onehot(owned, (hang, slots))).astype(I32)
    coarse_col = jnp.where(owned >= 0, 32 * found[0:1] + found[1:2], -1)
    slab, side = plane_ref[0], band_ref[0]
    repeat = jnp.where(
        jnp.bitwise_and(lanes((HALO, 128)), HALO - 1) == rows((HALO, 128)), 1.0, 0.0
    ).astype(BF16)
    halo = mm(
        stack_rows([slab[0:1], slab[1:2], side[0:1], side[1:2]], 16).astype(BF16), repeat
    ).astype(I32)
    group = jnp.right_shift(lanes((1, 128)), 4)
    halo_col = jnp.full((1, 128), -1, I32)
    for i in range(4):
        halo_col = jnp.where(group == i, halo[i : i + 1] + 128 * i, halo_col)
    oh_ref[:, 0:slots] = onehot(fine_col, (768, slots))
    oh_ref[:, slots : 2 * slots] = onehot(coarse_col, (768, slots))
    oh_ref[:, 2 * slots :] = onehot(halo_col, (768, 128))

    fine_w, coarse_w = fine_ref[...], coarse_ref[...]

    def masks(quadrant):
        return [jnp.where(quadrant == q, 1.0, 0.0).astype(BF16) for q in range(4)]

    out_masks, in_masks = masks(outq), masks(incq)

    def project(matrix, high, low, mask):
        def spread_out(part):
            part = part.astype(BF16)
            return jnp.concatenate([part * mask[q] for q in range(4)], axis=0)

        both = mm(matrix, spread_out(high))
        return both[:FACE] + both[FACE:] + mm(matrix[:FACE], spread_out(low))

    def send(step, u_traces):
        high, low = split(u_traces)
        tr_ref[0:FACE] = jnp.concatenate(
            [high[FACE * f : FACE * (f + 1)] for f in range(6)], axis=1
        )
        tr_ref[FACE:] = jnp.concatenate([low[FACE * f : FACE * (f + 1)] for f in range(6)], axis=1)
        gathered = mm(tr_ref[...], oh_ref[...])
        halo_out = gathered[:FACE, 2 * slots :] + gathered[FACE:, 2 * slots :]
        halo_out = jnp.concatenate([halo_out, jnp.zeros((48, 128), F32)], axis=0).T
        hx_ref[step] = halo_out[0 : 4 * HALO].reshape(4, HALO, 128)
        fine = project(fine_w, gathered[:FACE, :slots], gathered[FACE:, :slots], out_masks)
        coarse = project(
            coarse_w,
            gathered[:FACE, slots : 2 * slots],
            gathered[FACE:, slots : 2 * slots],
            in_masks,
        )
        rest = [coarse[HEAD:, half * c : half * c + half] for c in range(CAP)]
        blank = jnp.zeros((32, half), F32)
        tails = jnp.concatenate(
            [
                jnp.concatenate([rest[i], rest[4 + i] if i < 2 else blank], axis=1)
                for i in range(4)
            ],
            axis=0,
        )
        packed = jnp.concatenate(
            [jnp.concatenate([fine, coarse[:HEAD]], axis=0), tails], axis=1
        ).T
        for c in range(8):
            x_ref[step, pl.ds(c, n_yz, stride=8), :] = packed[n_yz * c : n_yz * c + n_yz]
        if step == 0:
            pl.semaphore_wait(barrier, n_yz + n_gx - 2)
        def one(m):
            pltpu.make_async_remote_copy(
                src_ref=x_ref.at[step, pl.ds(pl.multiple_of(8 * m, 8), 8)],
                dst_ref=recv_ref.at[step, mine],
                send_sem=send_sem.at[step, 1],
                recv_sem=recv_sem.at[step, 1],
                device_id=(g, m),
                device_id_type=MESH,
            ).start()

        plane(one)
        up_g, down_g = lax.rem(g + 1, n_gx), lax.rem(g + n_gx - 1, n_gx)
        up_k, down_k = lax.rem(k + 1, n_yz), lax.rem(k + n_yz - 1, n_yz)
        for source, target, device in (
            (0, 1, (down_g, k)),
            (1, 0, (up_g, k)),
            (2, 3, (g, down_k)),
            (3, 2, (g, up_k)),
        ):
            pltpu.make_async_remote_copy(
                src_ref=hx_ref.at[step, source],
                dst_ref=hrecv_ref.at[step, target],
                send_sem=send_sem.at[step, 0],
                recv_sem=recv_sem.at[step, 0],
                device_id=device,
                device_id_type=MESH,
            ).start()
        recv_ref[step, mine] = x_ref[step, mine]

    def halo_copy(step):
        return pltpu.make_async_remote_copy(
            src_ref=hx_ref.at[step],
            dst_ref=hrecv_ref.at[step],
            send_sem=send_sem.at[step, 0],
            recv_sem=recv_sem.at[step, 0],
            device_id=(g, k),
            device_id_type=MESH,
        )

    def plane_copy(step):
        return pltpu.make_async_remote_copy(
            src_ref=x_ref.at[step, pl.ds(0, wide - 8)],
            dst_ref=recv_ref.at[step, pl.ds(0, wide - 8)],
            send_sem=send_sem.at[step, 1],
            recv_sem=recv_sem.at[step, 1],
            device_id=(g, k),
            device_id_type=MESH,
        )

    def receive(step):
        halo_copy(step).wait_recv()
        plane_copy(step).wait_recv()
        tiles = jnp.concatenate(
            [recv_ref[step, pl.ds(c, n_yz, stride=8), :] for c in range(8)], axis=0
        ).T
        rest = jnp.concatenate(
            [
                tiles[
                    32 * (c % 4) : 32 * (c % 4) + 32,
                    half * (CAP + c // 4) : half * (CAP + c // 4) + half,
                ]
                for c in range(CAP)
            ],
            axis=1,
        )
        halo_in = hrecv_ref[step].reshape(4 * HALO, 128)
        at = jnp.right_shift(rows((4 * HALO, 128)), 4)
        drop = ((at == 0) & (g == 0)) | ((at == 1) & (g == n_gx - 1))
        halo_in = jnp.where(drop, 0.0, halo_in)
        halo_in = jnp.concatenate([halo_in, jnp.zeros((64, 128), F32)], axis=0).T[:FACE]
        values = jnp.concatenate(
            [
                tiles[:FACE, :slots],
                jnp.concatenate([tiles[FACE:, :slots], rest], axis=0),
                halo_in,
            ],
            axis=1,
        )
        high, low = split(values)
        near = mm(jnp.concatenate([high, low], axis=0), near_in_ref[...])
        return near[:FACE] + near[FACE:]

    def volume(u):
        high, low = split(u)
        node = node_ref[...]

        def by_variable(part):
            return jnp.concatenate([part[64 * v : 64 * v + 64] for v in range(5)], axis=1)

        high, low = by_variable(high), by_variable(low)
        slopes = mm(node, jnp.concatenate([high, low, high], axis=0))
        out = []
        for a in range(5):
            total = mass_ref[64 * a : 64 * a + 64] * u[64 * a : 64 * a + 64]
            for d in range(3):
                for v in range(5):
                    row = d * 25 + a * 5 + v
                    total = (
                        total
                        + flux_ref[row : row + 1]
                        * slopes[64 * d : 64 * d + 64, 128 * v : 128 * v + 128]
                    )
            out.append(total)
        return product(first, jnp.concatenate(out, axis=0))

    def own_near():
        near = mm(tr_ref[...], near_own_ref[...])
        return near[:FACE] + near[FACE:]

    def lifted(jumps):
        high, low = split(jumps)
        both = mm(lift_ref[0], jnp.concatenate([high, low], axis=1))
        return both[:, :128] + both[:, 128:] + mm(lift_ref[1], high)

    def finish(base, traces, near_own, near_in):
        near = near_own + near_in
        jumps = jnp.concatenate(
            [
                coef_ref[FACE * f : FACE * (f + 1)]
                * (traces[FACE * f : FACE * (f + 1)] - near[:, 128 * f : 128 * f + 128])
                for f in range(6)
            ],
            axis=0,
        )
        return (mid * SCALE) * (base + lifted(jumps))

    def fold(a, b):
        return jnp.sum(a * b, axis=0, keepdims=True)

    traces = product(pick_ref[...], weighted)
    send(0, traces)
    u_ref[0] = product(final, weighted)
    nt = (((1,), (1,)), ((), ()))
    lift_ref[0] = lax.dot_general(
        first_high, select, nt, preferred_element_type=F32
    ).astype(BF16)
    lift_ref[1] = lax.dot_general(
        first_low, select, nt, preferred_element_type=F32
    ).astype(BF16)
    ready("node", "mass", "flux", "coef", "adj")
    table = 768 + 4 * HALO
    owned_col = jnp.broadcast_to(jnp.where(owned >= 0, owned + table, -1), (128, slots)).T
    place = rows((slots, 128))
    reply = CAP * lax.rem(place, n_yz) + place // n_yz + table + hang
    halo_at = rows((128, 128))
    halo_at = jnp.where(halo_at < 4 * HALO, halo_at + 768, -1)
    for f in range(6):
        adj = adj_ref[f : f + 1]
        near_own_ref[:, 128 * f : 128 * f + 128] = onehot(adj, (768, 128))
        near_in_ref[0:slots, 128 * f : 128 * f + 128] = jnp.where(
            owned_col == adj, 1.0, 0.0
        ).astype(BF16)
        near_in_ref[slots : 2 * slots, 128 * f : 128 * f + 128] = jnp.where(
            reply == adj, 1.0, 0.0
        ).astype(BF16)
        near_in_ref[2 * slots :, 128 * f : 128 * f + 128] = jnp.where(
            halo_at == adj, 1.0, 0.0
        ).astype(BF16)
    base = volume(u_ref[0])
    near_own = own_near()
    weighted = finish(base, traces, near_own, receive(0))

    traces = product(pick_ref[...], weighted)
    send(1, traces)
    u_ref[1] = product(final, weighted)
    base = volume(u_ref[1])
    near_own = own_near()
    r, u1 = u_ref[0], u_ref[1]
    g00, g01, g11 = fold(r, r), fold(r, u1), fold(u1, u1)
    weighted = finish(base, traces, near_own, receive(1))
    u2 = product(final, weighted)

    gram = stack_rows([g00, g01, g11, fold(r, u2), fold(u1, u2), fold(u2, u2)], 8)
    column = jnp.sum(gram, axis=1, keepdims=True)
    gram = jnp.where(rows((8, 128)) == lanes((8, 128)), column, 0.0)
    gram = jnp.sum(gram, axis=0, keepdims=True)
    px_ref[...] = gram

    def one(m):
        pltpu.make_async_remote_copy(
            src_ref=px_ref,
            dst_ref=precv_ref.at[k],
            send_sem=send_sem.at[2, 1],
            recv_sem=recv_sem.at[2, 1],
            device_id=(g, m),
            device_id_type=MESH,
        ).start()

    plane(one)
    precv_ref[pl.ds(k, 1)] = gram.reshape(1, 1, 128)
    sum_copy = pltpu.make_async_remote_copy(
        src_ref=precv_ref.at[pl.ds(0, n_yz - 1)],
        dst_ref=precv_ref.at[pl.ds(0, n_yz - 1)],
        send_sem=send_sem.at[2, 1],
        recv_sem=recv_sem.at[2, 1],
        device_id=(g, k),
        device_id_type=MESH,
    )
    sum_copy.wait_recv()
    gram = jnp.sum(precv_ref[...], axis=0)
    gx_ref[...] = gram
    for partner_g in gx_partners:
        pltpu.make_async_remote_copy(
            src_ref=gx_ref,
            dst_ref=grecv_ref.at[g],
            send_sem=send_sem.at[2, 0],
            recv_sem=recv_sem.at[2, 0],
            device_id=(partner_g, k),
            device_id_type=MESH,
        ).start()
    grecv_ref[pl.ds(g, 1)] = gram.reshape(1, 1, 128)
    gram_copy = pltpu.make_async_remote_copy(
        src_ref=grecv_ref.at[pl.ds(0, n_gx - 1)],
        dst_ref=grecv_ref.at[pl.ds(0, n_gx - 1)],
        send_sem=send_sem.at[2, 0],
        recv_sem=recv_sem.at[2, 0],
        device_id=(g, k),
        device_id_type=MESH,
    )
    gram_copy.wait_recv()
    total = jnp.sum(grecv_ref[...], axis=0)
    at = lanes((1, 128))

    def entry(i):
        return jnp.sum(jnp.where(at == i, total, 0.0), axis=1, keepdims=True)

    c_r, c_u = coefficients(*[entry(i) for i in range(6)])
    out_ref[...] = c_r * u_ref[0] + c_u * u_ref[1]

    for step in range(2):
        halo_copy(step).wait_send()
        plane_copy(step).wait_send()
    gram_copy.wait_send()
    sum_copy.wait_send()


def coefficients(g00, g01, g11, g02, g12, g22):
    s = SCALE
    beta = jnp.sqrt(g00 + EPSILON)
    h00 = g01 / (s * beta * beta)
    p1, p0 = 1.0 / s, -h00
    norm = (p1 * p1 * g11 + 2.0 * p1 * p0 * g01 + p0 * p0 * g00) / (beta * beta)
    h10 = jnp.sqrt(jnp.maximum(norm, 0.0) + EPSILON)
    c1, c0 = p1 / (beta * h10), p0 / (beta * h10)
    a2, a1 = c1 / s, c0 / s
    h01 = (a2 * g02 + a1 * g01) / beta
    a0 = -h01 / beta
    h11 = c1 * (a2 * g12 + a1 * g11 + a0 * g01) + c0 * (a2 * g02 + a1 * g01 + a0 * g00)
    a1, a0 = a1 - h11 * c1, a0 - h11 * c0
    norm = a2 * (a2 * g22 + 2.0 * (a1 * g12 + a0 * g02)) + (
        a1 * (a1 * g11 + 2.0 * a0 * g01) + a0 * a0 * g00
    )
    h21 = jnp.sqrt(jnp.maximum(norm, 0.0) + EPSILON)
    radius = jnp.sqrt(h00 * h00 + h10 * h10)
    cos0, sin0 = h00 / radius, h10 / radius
    top = cos0 * h01 + sin0 * h11
    low = cos0 * h11 - sin0 * h01
    length = jnp.sqrt(low * low + h21 * h21)
    y1 = (low / length) * (-sin0 * beta) / length
    y0 = (cos0 * beta - top * y1) / radius
    return y0 / beta + y1 * c0, y1 * c1


def on_device(
    n_gx,
    n_yz,
    source,
    mass,
    coupling,
    flux,
    first,
    final,
    middle,
    adjacent,
    plane,
    band,
    small,
    proprietor,
    outq,
    incm,
    incq,
    cmts,
):
    del proprietor
    tables = [jnp.asarray(t) for t in gll_tables()]
    wide, slots = 8 * n_yz, CAP * n_yz
    arguments = (
        source, mass, coupling, flux, first, final, middle, adjacent, plane, band,
        small, outq, incm, incq, cmts, *tables,
    )
    vmem = pl.BlockSpec(memory_space=pltpu.VMEM)
    hbm = pl.BlockSpec(memory_space=pltpu.HBM)
    return pl.pallas_call(
        functools.partial(kernel, n_gx, n_yz, cmts.shape[1]),
        out_shape=jax.ShapeDtypeStruct(source.shape, F32),
        in_specs=[hbm] * len(arguments),
        out_specs=vmem,
        scratch_shapes=[
            *[pltpu.VMEM(a.shape, a.dtype) for a in arguments],
            pltpu.SemaphoreType.DMA((len(arguments),)),
            pltpu.VMEM((2, wide, 128), F32),
            pltpu.VMEM((2, wide, 128), F32),
            pltpu.VMEM((2, 4, HALO, 128), F32),
            pltpu.VMEM((2, 4, HALO, 128), F32),
            pltpu.VMEM((1, 128), F32),
            pltpu.VMEM((n_gx, 1, 128), F32),
            pltpu.VMEM((1, 128), F32),
            pltpu.VMEM((n_yz, 1, 128), F32),
            pltpu.VMEM((768, 2 * slots + 128), BF16),
            pltpu.VMEM((768, 768), BF16),
            pltpu.VMEM((2 * slots + 128, 768), BF16),
            pltpu.VMEM((480, 640), BF16),
            pltpu.VMEM((2, 320, 480), BF16),
            pltpu.VMEM((2 * FACE, 768), BF16),
            pltpu.VMEM((2, 320, 128), F32),
            pltpu.SemaphoreType.DMA((3, 2)),
            pltpu.SemaphoreType.DMA((3, 2)),
        ],
        compiler_params=pltpu.CompilerParams(
            collective_id=0, has_side_effects=True, vmem_limit_bytes=63 * 1024 * 1024
        ),
    )(*arguments)


def solution(mesh):
    n_gx, n_yz = mesh.shape["gx"], mesh.shape["yz"]
    both = ("gx", "yz")
    field, lists = P(None, both), P(both, None)
    return jax.shard_map(
        functools.partial(on_device, n_gx, n_yz),
        mesh=mesh,
        in_specs=(
            field, field, field, field, P(), P(), field, field,
            P(both, None, None), P(both, None, None),
            lists, lists, lists, lists, lists, lists,
        ),
        out_specs=field,
        check_vma=False,
    )
```

```python
import functools

import jax
import jax.numpy as jnp
import ml_dtypes
import numpy as np
from jax import lax
from jax.experimental import pallas as pl
from jax.experimental.pallas import tpu as pltpu
from jax.sharding import PartitionSpec as P

MESH = pl.DeviceIdType.MESH
F32 = jnp.float32
BF16 = jnp.bfloat16
I32 = jnp.int32

EPSILON = 1e-6
SCALE = 2.0**-10
CAP = 6
FACE = 80
HALO = 16
HEAD = 128 - FACE


def split_np(array):
    high = array.astype(np.float32).astype(ml_dtypes.bfloat16)
    low = (array - high.astype(np.float64)).astype(np.float32).astype(ml_dtypes.bfloat16)
    return high, low


def gll_tables():
    inv_root = 1.0 / np.sqrt(5.0)
    points = np.array([-1.0, -inv_root, inv_root, 1.0])
    weights = np.array([1.0, 5.0, 5.0, 1.0]) / 6.0

    def lagrange(at):
        values = np.ones((len(at), 4))
        for j in range(4):
            for m in range(4):
                if m != j:
                    values[:, j] = values[:, j] * (at - points[m]) / (points[j] - points[m])
        return values

    derivative = np.zeros((4, 4))
    for i in range(4):
        for j in range(4):
            for m in range(4):
                if m != j:
                    term = 1.0 / (points[j] - points[m])
                    for n in range(4):
                        if n != j and n != m:
                            term = term * (points[i] - points[n]) / (points[j] - points[n])
                    derivative[i, j] += term
    halves = [lagrange((points - 1.0) / 2.0), lagrange((points + 1.0) / 2.0)]
    projections = [0.5 * (1.0 / weights)[:, None] * h.T * weights[None, :] for h in halves]
    one5, one4 = np.eye(5), np.eye(4)
    fine = np.concatenate(
        [np.kron(one5, np.kron(projections[q // 2], projections[q % 2])) for q in range(4)], axis=1
    )
    coarse = np.concatenate(
        [np.kron(one5, np.kron(halves[q // 2], halves[q % 2])) for q in range(4)], axis=1
    )
    node = np.concatenate(
        [
            np.kron(derivative, np.kron(one4, one4)),
            np.kron(one4, np.kron(derivative, one4)),
            np.kron(one4, np.kron(one4, derivative)),
        ],
        axis=0,
    )
    select = np.zeros((6, FACE, 320))
    for face in range(6):
        fixed = 3 * (face % 2)
        for a in range(5):
            for p in range(4):
                for q in range(4):
                    n = (
                        fixed * 16 + p * 4 + q,
                        p * 16 + fixed * 4 + q,
                        p * 16 + q * 4 + fixed,
                    )[face // 2]
                    select[face, a * 16 + p * 4 + q, a * 64 + n] = 1.0
    node_high, node_low = split_np(node)
    return (
        np.concatenate([node_high, node_high, node_low], axis=1),
        np.concatenate(split_np(fine), axis=0),
        np.concatenate(split_np(coarse), axis=0),
        select.reshape(480, 320).astype(ml_dtypes.bfloat16),
    )


def split(array):
    high = array.astype(BF16)
    return high, (array - high.astype(F32)).astype(BF16)


def mm(a, b):
    return jnp.dot(a, b, preferred_element_type=F32)


def side_by_side(high, low):
    return jnp.concatenate([high[:, :256], low[:, :256], high[:, 256:], low[:, 256:]], axis=1)


def product(a, b):
    high, low = split(b)
    blank = jnp.zeros_like(low)
    both = mm(
        a,
        jnp.concatenate(
            [
                jnp.concatenate([high[:256], high[:256], high[256:], high[256:]], axis=0),
                jnp.concatenate([low[:256], blank[:256], low[256:], blank[256:]], axis=0),
            ],
            axis=1,
        ),
    )
    n = b.shape[1]
    return both[:, :n] + both[:, n:]


def lanes(shape):
    return lax.broadcasted_iota(I32, shape, 1)


def rows(shape):
    return lax.broadcasted_iota(I32, shape, 0)


def stack_rows(parts, count):
    shape = (count, parts[0].shape[1])
    at = rows(shape)
    out = jnp.zeros(shape, F32)
    for i, part in enumerate(parts):
        out = jnp.where(at == i, part.astype(F32), out)
    return out


def onehot(index, shape):
    return jnp.where(index == rows(shape), 1.0, 0.0).astype(BF16)


def far_first(size):
    return sorted(range(size), key=lambda d: -min(d, size - d))


def outward(i, size):
    return lax.rem(size // 2 + (i + 1) // 2 * (1 - 2 * lax.rem(i, 2)) + size, size)


def kernel(
    n_gx,
    n_yz,
    hang,
    b_hbm,
    mass_hbm,
    coef_hbm,
    flux_hbm,
    first_hbm,
    final_hbm,
    mid_hbm,
    adj_hbm,
    plane_hbm,
    band_hbm,
    small_hbm,
    outq_hbm,
    incm_hbm,
    incq_hbm,
    cmts_hbm,
    node_hbm,
    fine_hbm,
    coarse_hbm,
    select_hbm,
    out_ref,
    b_ref,
    mass_ref,
    coef_ref,
    flux_ref,
    first_ref,
    final_ref,
    mid_ref,
    adj_ref,
    plane_ref,
    band_ref,
    small_ref,
    outq_ref,
    incm_ref,
    incq_ref,
    cmts_ref,
    node_ref,
    fine_ref,
    coarse_ref,
    select_ref,
    load_sem,
    x_ref,
    recv_ref,
    hx_ref,
    hrecv_ref,
    gx_ref,
    grecv_ref,
    px_ref,
    precv_ref,
    oh_ref,
    near_own_ref,
    near_in_ref,
    pick_ref,
    lift_ref,
    tr_ref,
    u_ref,
    send_sem,
    recv_sem,
):
    g, k = lax.axis_index("gx"), lax.axis_index("yz")
    wide = 8 * n_yz
    slots = CAP * n_yz
    barrier = pltpu.get_barrier_semaphore()

    n_y = 8 if n_yz % 16 == 0 else n_yz // 2
    n_x = n_yz // (2 * n_y)
    x, y, core = k // (2 * n_y), lax.rem(k // 2, n_y), lax.rem(k, 2)

    columns = [
        (lax.rem(x + dx, n_x) * n_y * 2, dx, c)
        for dx in far_first(n_x)
        for c in (1, 0)
    ]
    cores = (core, 1 - core)

    def plane(act, start=0, end=n_y):
        def one(i, _):
            at = lax.rem(y + outward(i, n_y), n_y) * 2
            for r, (column, _, c) in enumerate(columns):
                act(column + at + cores[c], i * 2 * n_x + r)
            return 0

        lax.fori_loop(start, min(end, n_y - 1), one, 0)
        if end == n_y:
            for r, (column, dx, c) in enumerate(columns):
                if dx or c:
                    act(column + y * 2 + cores[c], (n_y - 1) * 2 * n_x + r)

    mine = pl.ds(pl.multiple_of(8 * k, 8), 8)

    def greet(device, _):
        pl.semaphore_signal(barrier, inc=1, device_id=(g, device), device_id_type=MESH)

    plane(greet)
    gx_partners = [lax.rem(g + dg, n_gx) for dg in far_first(n_gx) if dg]
    for partner_g in gx_partners:
        pl.semaphore_signal(barrier, inc=1, device_id=(partner_g, k), device_id_type=MESH)
    loads = {}
    for i, (name, source, target) in enumerate(
        (
            ("first", first_hbm, first_ref),
            ("b", b_hbm, b_ref),
            ("small", small_hbm, small_ref),
            ("outq", outq_hbm, outq_ref),
            ("incm", incm_hbm, incm_ref),
            ("incq", incq_hbm, incq_ref),
            ("cmts", cmts_hbm, cmts_ref),
            ("plane", plane_hbm, plane_ref),
            ("band", band_hbm, band_ref),
            ("mid", mid_hbm, mid_ref),
            ("final", final_hbm, final_ref),
            ("select", select_hbm, select_ref),
            ("fine", fine_hbm, fine_ref),
            ("coarse", coarse_hbm, coarse_ref),
            ("node", node_hbm, node_ref),
            ("mass", mass_hbm, mass_ref),
            ("flux", flux_hbm, flux_ref),
            ("coef", coef_hbm, coef_ref),
            ("adj", adj_hbm, adj_ref),
        )
    ):
        loads[name] = pltpu.make_async_copy(source, target, load_sem.at[i])
        loads[name].start()

    def ready(*wanted):
        for name in wanted:
            loads[name].wait()

    half = n_yz // 2
    part = 8 * half
    place = lanes((1, 2 * part))
    place_c = lax.rem(place, part) // half
    place_i = (place // part) * half + lax.rem(place, half)
    jx = lax.rem(place_i, 2 * n_x) // 2
    place_x = jnp.zeros_like(jx)
    for j, dx in enumerate(far_first(n_x)):
        place_x = jnp.where(jx == j, dx, place_x)
    place_x = lax.rem(x + place_x, n_x)
    place_y = lax.rem(y + outward(place_i // (2 * n_x), n_y), n_y)
    place_core = lax.rem(core + 1 + place_i, 2)
    place_device = (place_x * n_y + place_y) * 2 + place_core

    ready("first", "b", "small", "outq", "incm", "incq", "cmts", "plane", "band")
    ready("mid", "final", "select", "fine", "coarse")
    first_high, first_low = split(first_ref[...])
    final_high, final_low = split(final_ref[...])
    first = side_by_side(first_high, first_low)
    final = side_by_side(final_high, final_low)
    select = select_ref[...]
    pick_ref[...] = mm(select, final).astype(BF16)

    mid = mid_ref[...]
    weighted = mid * product(first, b_ref[...])

    small = small_ref[...]
    incm = incm_ref[...]
    parts = [
        jnp.right_shift(small, 5),
        jnp.bitwise_and(small, 31),
        outq_ref[...],
        incm,
        incq_ref[...],
    ]
    live = place_c < CAP
    target = jnp.where(live, CAP * place_device + place_c, -1)
    spread = mm(stack_rows(parts, 16).astype(BF16), onehot(target, (slots, 2 * part)))
    spread = spread.astype(I32)
    fine_col = jnp.where(live, 32 * spread[0:1] + spread[1:2], -1)
    outq = spread[2:3]
    asked = jnp.where(live & (spread[3:4] < hang), spread[3:4], -1)
    incq = spread[4:5]
    cmts = cmts_ref[...]
    parts = [jnp.right_shift(cmts, 5), jnp.bitwise_and(cmts, 31)]
    found = mm(stack_rows(parts, 16).astype(BF16), onehot(asked, (hang, 2 * part))).astype(I32)
    coarse_col = jnp.where(asked >= 0, 32 * found[0:1] + found[1:2], -1)
    slab, side = plane_ref[0], band_ref[0]
    repeat = jnp.where(
        jnp.bitwise_and(lanes((HALO, 128)), HALO - 1) == rows((HALO, 128)), 1.0, 0.0
    ).astype(BF16)
    halo = mm(
        stack_rows([slab[0:1], slab[1:2], side[0:1], side[1:2]], 16).astype(BF16), repeat
    ).astype(I32)
    group = jnp.right_shift(lanes((1, 128)), 4)
    halo_col = jnp.full((1, 128), -1, I32)
    for i in range(4):
        halo_col = jnp.where(group == i, halo[i : i + 1] + 128 * i, halo_col)
    for i in range(2):
        cut = slice(part * i, part * i + part)
        at = 2 * part * i
        oh_ref[:, at : at + part] = onehot(fine_col[:, cut], (768, part))
        oh_ref[:, at + part : at + 2 * part] = onehot(coarse_col[:, cut], (768, part))
    oh_ref[:, 4 * part :] = onehot(halo_col, (768, 128))

    fine_w, coarse_w = fine_ref[...], coarse_ref[...]

    def masks(quadrant):
        return [jnp.where(quadrant == q, 1.0, 0.0).astype(BF16) for q in range(4)]

    out_masks, in_masks = masks(outq), masks(incq)

    def project(matrix, high, low, mask):
        def spread_out(values):
            values = values.astype(BF16)
            return jnp.concatenate([values * mask[q] for q in range(4)], axis=0)

        both = mm(matrix, spread_out(high))
        return both[:FACE] + both[FACE:] + mm(matrix[:FACE], spread_out(low))

    def send_part(step, i):
        cut = slice(part * i, part * i + part)
        gathered = mm(tr_ref[...], oh_ref[:, 2 * part * i : 2 * part * i + 2 * part])
        fine = project(
            fine_w, gathered[:FACE, :part], gathered[FACE:, :part], [m[:, cut] for m in out_masks]
        )
        coarse = project(
            coarse_w, gathered[:FACE, part:], gathered[FACE:, part:], [m[:, cut] for m in in_masks]
        )
        rest = [coarse[HEAD:, half * c : half * c + half] for c in range(CAP)]
        blank = jnp.zeros((32, half), F32)
        tails = jnp.concatenate(
            [
                jnp.concatenate([rest[j], rest[4 + j] if j < 2 else blank], axis=1)
                for j in range(4)
            ],
            axis=0,
        )
        head = jnp.concatenate([fine[:, : CAP * half], coarse[:HEAD, : CAP * half]], axis=0)
        packed = jnp.concatenate([head, tails], axis=1).T
        for c in range(8):
            x_ref[step, i, pl.ds(c, half, stride=8), :] = packed[
                half * c : half * c + half
            ]

    def start_part(step, i, start, end):
        def one(m, at):
            pltpu.make_async_remote_copy(
                src_ref=x_ref.at[step, i, pl.ds(pl.multiple_of(8 * at - part * i, 8), 8)],
                dst_ref=recv_ref.at[step, mine],
                send_sem=send_sem.at[step, 1],
                recv_sem=recv_sem.at[step, 1],
                device_id=(g, m),
                device_id_type=MESH,
            ).start()

        plane(one, start, end)

    def send(step, u_traces):
        high, low = split(u_traces)
        tr_ref[0:FACE] = jnp.concatenate(
            [high[FACE * f : FACE * (f + 1)] for f in range(6)], axis=1
        )
        tr_ref[FACE:] = jnp.concatenate([low[FACE * f : FACE * (f + 1)] for f in range(6)], axis=1)
        send_part(step, 0)
        if step == 0:
            pl.semaphore_wait(barrier, n_yz + n_gx - 2)
        start_part(step, 0, 0, n_y // 2)
        send_part(step, 1)
        start_part(step, 1, n_y // 2, n_y)
        halo_out = mm(tr_ref[...], oh_ref[:, 4 * part :])
        halo_out = halo_out[:FACE] + halo_out[FACE:]
        halo_out = jnp.concatenate([halo_out, jnp.zeros((48, 128), F32)], axis=0).T
        hx_ref[step] = halo_out[0 : 4 * HALO].reshape(4, HALO, 128)
        up_g, down_g = lax.rem(g + 1, n_gx), lax.rem(g + n_gx - 1, n_gx)
        up_k, down_k = lax.rem(k + 1, n_yz), lax.rem(k + n_yz - 1, n_yz)
        for source, target, device in (
            (0, 1, (down_g, k)),
            (1, 0, (up_g, k)),
            (2, 3, (g, down_k)),
            (3, 2, (g, up_k)),
        ):
            pltpu.make_async_remote_copy(
                src_ref=hx_ref.at[step, source],
                dst_ref=hrecv_ref.at[step, target],
                send_sem=send_sem.at[step, 0],
                recv_sem=recv_sem.at[step, 0],
                device_id=device,
                device_id_type=MESH,
            ).start()
        recv_ref[step, mine] = x_ref[step, 1, pl.ds(part - 8, 8)]

    def halo_copy(step):
        return pltpu.make_async_remote_copy(
            src_ref=hx_ref.at[step],
            dst_ref=hrecv_ref.at[step],
            send_sem=send_sem.at[step, 0],
            recv_sem=recv_sem.at[step, 0],
            device_id=(g, k),
            device_id_type=MESH,
        )

    def plane_copy(step):
        return pltpu.make_async_remote_copy(
            src_ref=recv_ref.at[step, pl.ds(0, wide - 8)],
            dst_ref=recv_ref.at[step, pl.ds(0, wide - 8)],
            send_sem=send_sem.at[step, 1],
            recv_sem=recv_sem.at[step, 1],
            device_id=(g, k),
            device_id_type=MESH,
        )

    def receive(step):
        halo_copy(step).wait_recv()
        plane_copy(step).wait_recv()
        tiles = jnp.concatenate(
            [recv_ref[step, pl.ds(c, n_yz, stride=8), :] for c in range(8)], axis=0
        ).T
        rest = jnp.concatenate(
            [
                tiles[
                    32 * (c % 4) : 32 * (c % 4) + 32,
                    n_yz * (CAP + c // 4) : n_yz * (CAP + c // 4) + n_yz,
                ]
                for c in range(CAP)
            ],
            axis=1,
        )
        halo_in = hrecv_ref[step].reshape(4 * HALO, 128)
        at = jnp.right_shift(rows((4 * HALO, 128)), 4)
        drop = ((at == 0) & (g == 0)) | ((at == 1) & (g == n_gx - 1))
        halo_in = jnp.where(drop, 0.0, halo_in)
        halo_in = jnp.concatenate([halo_in, jnp.zeros((64, 128), F32)], axis=0).T[:FACE]
        values = jnp.concatenate(
            [
                tiles[:FACE, :slots],
                jnp.concatenate([tiles[FACE:, :slots], rest], axis=0),
                halo_in,
            ],
            axis=1,
        )
        high, low = split(values)
        near = mm(jnp.concatenate([high, low], axis=0), near_in_ref[...])
        return near[:FACE] + near[FACE:]

    def volume(u):
        high, low = split(u)
        node = node_ref[...]

        def by_variable(part):
            return jnp.concatenate([part[64 * v : 64 * v + 64] for v in range(5)], axis=1)

        high, low = by_variable(high), by_variable(low)
        slopes = mm(node, jnp.concatenate([high, low, high], axis=0))
        out = []
        for a in range(5):
            total = mass_ref[64 * a : 64 * a + 64] * u[64 * a : 64 * a + 64]
            for d in range(3):
                for v in range(5):
                    row = d * 25 + a * 5 + v
                    total = (
                        total
                        + flux_ref[row : row + 1]
                        * slopes[64 * d : 64 * d + 64, 128 * v : 128 * v + 128]
                    )
            out.append(total)
        return product(first, jnp.concatenate(out, axis=0))

    def own_near():
        near = mm(tr_ref[...], near_own_ref[...])
        return near[:FACE] + near[FACE:]

    def lifted(jumps):
        high, low = split(jumps)
        both = mm(lift_ref[0], jnp.concatenate([high, low], axis=1))
        return both[:, :128] + both[:, 128:] + mm(lift_ref[1], high)

    def finish(base, traces, near_own, near_in):
        near = near_own + near_in
        jumps = jnp.concatenate(
            [
                coef_ref[FACE * f : FACE * (f + 1)]
                * (traces[FACE * f : FACE * (f + 1)] - near[:, 128 * f : 128 * f + 128])
                for f in range(6)
            ],
            axis=0,
        )
        return (mid * SCALE) * (base + lifted(jumps))

    def fold(a, b):
        return jnp.sum(a * b, axis=0, keepdims=True)

    traces = product(pick_ref[...], weighted)
    send(0, traces)
    u_ref[0] = product(final, weighted)
    nt = (((1,), (1,)), ((), ()))
    lift_ref[0] = lax.dot_general(
        first_high, select, nt, preferred_element_type=F32
    ).astype(BF16)
    lift_ref[1] = lax.dot_general(
        first_low, select, nt, preferred_element_type=F32
    ).astype(BF16)
    ready("node", "mass", "flux", "coef", "adj")
    table = 768 + 4 * HALO
    lane = lanes((1, slots))
    natural = CAP * lax.rem(lane, n_yz) + lane // n_yz
    owned = mm(stack_rows([incm], 16).astype(BF16), onehot(natural, (slots, slots)))[0:1]
    owned = owned.astype(I32)
    owned = jnp.where(owned < hang, owned + table, -1)
    owned_col = jnp.broadcast_to(owned, (128, slots)).T
    slot = rows((slots, 128))
    reply = CAP * lax.rem(slot, n_yz) + slot // n_yz + table + hang
    halo_at = rows((128, 128))
    halo_at = jnp.where(halo_at < 4 * HALO, halo_at + 768, -1)
    for f in range(6):
        adj = adj_ref[f : f + 1]
        near_own_ref[:, 128 * f : 128 * f + 128] = onehot(adj, (768, 128))
        near_in_ref[0:slots, 128 * f : 128 * f + 128] = jnp.where(
            owned_col == adj, 1.0, 0.0
        ).astype(BF16)
        near_in_ref[slots : 2 * slots, 128 * f : 128 * f + 128] = jnp.where(
            reply == adj, 1.0, 0.0
        ).astype(BF16)
        near_in_ref[2 * slots :, 128 * f : 128 * f + 128] = jnp.where(
            halo_at == adj, 1.0, 0.0
        ).astype(BF16)
    base = volume(u_ref[0])
    near_own = own_near()
    weighted = finish(base, traces, near_own, receive(0))

    traces = product(pick_ref[...], weighted)
    send(1, traces)
    u_ref[1] = product(final, weighted)
    base = volume(u_ref[1])
    near_own = own_near()
    r, u1 = u_ref[0], u_ref[1]
    g00, g01, g11 = fold(r, r), fold(r, u1), fold(u1, u1)
    weighted = finish(base, traces, near_own, receive(1))
    u2 = product(final, weighted)

    gram = stack_rows([g00, g01, g11, fold(r, u2), fold(u1, u2), fold(u2, u2)], 8)
    column = jnp.sum(gram, axis=1, keepdims=True)
    gram = jnp.where(rows((8, 128)) == lanes((8, 128)), column, 0.0)
    gram = jnp.sum(gram, axis=0, keepdims=True)
    px_ref[...] = gram

    def one(m, _):
        pltpu.make_async_remote_copy(
            src_ref=px_ref,
            dst_ref=precv_ref.at[k],
            send_sem=send_sem.at[2, 1],
            recv_sem=recv_sem.at[2, 1],
            device_id=(g, m),
            device_id_type=MESH,
        ).start()

    plane(one)
    precv_ref[pl.ds(k, 1)] = gram.reshape(1, 1, 128)
    sum_copy = pltpu.make_async_remote_copy(
        src_ref=precv_ref.at[pl.ds(0, n_yz - 1)],
        dst_ref=precv_ref.at[pl.ds(0, n_yz - 1)],
        send_sem=send_sem.at[2, 1],
        recv_sem=recv_sem.at[2, 1],
        device_id=(g, k),
        device_id_type=MESH,
    )
    sum_copy.wait_recv()
    gram = jnp.sum(precv_ref[...], axis=0)
    gx_ref[...] = gram
    for partner_g in gx_partners:
        pltpu.make_async_remote_copy(
            src_ref=gx_ref,
            dst_ref=grecv_ref.at[g],
            send_sem=send_sem.at[2, 0],
            recv_sem=recv_sem.at[2, 0],
            device_id=(partner_g, k),
            device_id_type=MESH,
        ).start()
    grecv_ref[pl.ds(g, 1)] = gram.reshape(1, 1, 128)
    gram_copy = pltpu.make_async_remote_copy(
        src_ref=grecv_ref.at[pl.ds(0, n_gx - 1)],
        dst_ref=grecv_ref.at[pl.ds(0, n_gx - 1)],
        send_sem=send_sem.at[2, 0],
        recv_sem=recv_sem.at[2, 0],
        device_id=(g, k),
        device_id_type=MESH,
    )
    gram_copy.wait_recv()
    total = jnp.sum(grecv_ref[...], axis=0)
    at = lanes((1, 128))

    def entry(i):
        return jnp.sum(jnp.where(at == i, total, 0.0), axis=1, keepdims=True)

    c_r, c_u = coefficients(*[entry(i) for i in range(6)])
    out_ref[...] = c_r * u_ref[0] + c_u * u_ref[1]

    for step in range(2):
        halo_copy(step).wait_send()
        plane_copy(step).wait_send()
    gram_copy.wait_send()
    sum_copy.wait_send()


def coefficients(g00, g01, g11, g02, g12, g22):
    s = SCALE
    beta = jnp.sqrt(g00 + EPSILON)
    h00 = g01 / (s * beta * beta)
    p1, p0 = 1.0 / s, -h00
    norm = (p1 * p1 * g11 + 2.0 * p1 * p0 * g01 + p0 * p0 * g00) / (beta * beta)
    h10 = jnp.sqrt(jnp.maximum(norm, 0.0) + EPSILON)
    c1, c0 = p1 / (beta * h10), p0 / (beta * h10)
    a2, a1 = c1 / s, c0 / s
    h01 = (a2 * g02 + a1 * g01) / beta
    a0 = -h01 / beta
    h11 = c1 * (a2 * g12 + a1 * g11 + a0 * g01) + c0 * (a2 * g02 + a1 * g01 + a0 * g00)
    a1, a0 = a1 - h11 * c1, a0 - h11 * c0
    norm = a2 * (a2 * g22 + 2.0 * (a1 * g12 + a0 * g02)) + (
        a1 * (a1 * g11 + 2.0 * a0 * g01) + a0 * a0 * g00
    )
    h21 = jnp.sqrt(jnp.maximum(norm, 0.0) + EPSILON)
    radius = jnp.sqrt(h00 * h00 + h10 * h10)
    cos0, sin0 = h00 / radius, h10 / radius
    top = cos0 * h01 + sin0 * h11
    low = cos0 * h11 - sin0 * h01
    length = jnp.sqrt(low * low + h21 * h21)
    y1 = (low / length) * (-sin0 * beta) / length
    y0 = (cos0 * beta - top * y1) / radius
    return y0 / beta + y1 * c0, y1 * c1


def on_device(
    n_gx,
    n_yz,
    source,
    mass,
    coupling,
    flux,
    first,
    final,
    middle,
    adjacent,
    plane,
    band,
    small,
    proprietor,
    outq,
    incm,
    incq,
    cmts,
):
    del proprietor
    tables = [jnp.asarray(t) for t in gll_tables()]
    wide, slots = 8 * n_yz, CAP * n_yz
    arguments = (
        source, mass, coupling, flux, first, final, middle, adjacent, plane, band,
        small, outq, incm, incq, cmts, *tables,
    )
    vmem = pl.BlockSpec(memory_space=pltpu.VMEM)
    hbm = pl.BlockSpec(memory_space=pltpu.HBM)
    return pl.pallas_call(
        functools.partial(kernel, n_gx, n_yz, cmts.shape[1]),
        out_shape=jax.ShapeDtypeStruct(source.shape, F32),
        in_specs=[hbm] * len(arguments),
        out_specs=vmem,
        scratch_shapes=[
            *[pltpu.VMEM(a.shape, a.dtype) for a in arguments],
            pltpu.SemaphoreType.DMA((len(arguments),)),
            pltpu.VMEM((2, 2, wide // 2, 128), F32),
            pltpu.VMEM((2, wide, 128), F32),
            pltpu.VMEM((2, 4, HALO, 128), F32),
            pltpu.VMEM((2, 4, HALO, 128), F32),
            pltpu.VMEM((1, 128), F32),
            pltpu.VMEM((n_gx, 1, 128), F32),
            pltpu.VMEM((1, 128), F32),
            pltpu.VMEM((n_yz, 1, 128), F32),
            pltpu.VMEM((768, 4 * wide // 2 + 128), BF16),
            pltpu.VMEM((768, 768), BF16),
            pltpu.VMEM((2 * slots + 128, 768), BF16),
            pltpu.VMEM((480, 640), BF16),
            pltpu.VMEM((2, 320, 480), BF16),
            pltpu.VMEM((2 * FACE, 768), BF16),
            pltpu.VMEM((2, 320, 128), F32),
            pltpu.SemaphoreType.DMA((3, 2)),
            pltpu.SemaphoreType.DMA((3, 2)),
        ],
        compiler_params=pltpu.CompilerParams(
            collective_id=0, has_side_effects=True, vmem_limit_bytes=63 * 1024 * 1024
        ),
    )(*arguments)


def solution(mesh):
    n_gx, n_yz = mesh.shape["gx"], mesh.shape["yz"]
    both = ("gx", "yz")
    field, lists = P(None, both), P(both, None)
    return jax.shard_map(
        functools.partial(on_device, n_gx, n_yz),
        mesh=mesh,
        in_specs=(
            field, field, field, field, P(), P(), field, field,
            P(both, None, None), P(both, None, None),
            lists, lists, lists, lists, lists, lists,
        ),
        out_specs=field,
        check_vma=False,
    )
```

```python
import functools

import jax
import jax.numpy as jnp
import ml_dtypes
import numpy as np
from jax import lax
from jax.experimental import pallas as pl
from jax.experimental.pallas import tpu as pltpu
from jax.sharding import PartitionSpec as P

MESH = pl.DeviceIdType.MESH
F32 = jnp.float32
BF16 = jnp.bfloat16
I32 = jnp.int32

EPSILON = 1e-6
SCALE = 2.0**-10
CAP = 6
FACE = 80
HALO = 16
HEAD = 128 - FACE


def split_np(array):
    high = array.astype(np.float32).astype(ml_dtypes.bfloat16)
    low = (array - high.astype(np.float64)).astype(np.float32).astype(ml_dtypes.bfloat16)
    return high, low


def gll_tables():
    inv_root = 1.0 / np.sqrt(5.0)
    points = np.array([-1.0, -inv_root, inv_root, 1.0])
    weights = np.array([1.0, 5.0, 5.0, 1.0]) / 6.0

    def lagrange(at):
        values = np.ones((len(at), 4))
        for j in range(4):
            for m in range(4):
                if m != j:
                    values[:, j] = values[:, j] * (at - points[m]) / (points[j] - points[m])
        return values

    derivative = np.zeros((4, 4))
    for i in range(4):
        for j in range(4):
            for m in range(4):
                if m != j:
                    term = 1.0 / (points[j] - points[m])
                    for n in range(4):
                        if n != j and n != m:
                            term = term * (points[i] - points[n]) / (points[j] - points[n])
                    derivative[i, j] += term
    halves = [lagrange((points - 1.0) / 2.0), lagrange((points + 1.0) / 2.0)]
    projections = [0.5 * (1.0 / weights)[:, None] * h.T * weights[None, :] for h in halves]
    one5, one4 = np.eye(5), np.eye(4)
    fine = np.concatenate(
        [np.kron(one5, np.kron(projections[q // 2], projections[q % 2])) for q in range(4)], axis=1
    )
    coarse = np.concatenate(
        [np.kron(one5, np.kron(halves[q // 2], halves[q % 2])) for q in range(4)], axis=1
    )
    node = np.concatenate(
        [
            np.kron(derivative, np.kron(one4, one4)),
            np.kron(one4, np.kron(derivative, one4)),
            np.kron(one4, np.kron(one4, derivative)),
        ],
        axis=0,
    )
    select = np.zeros((6, FACE, 320))
    for face in range(6):
        fixed = 3 * (face % 2)
        for a in range(5):
            for p in range(4):
                for q in range(4):
                    n = (
                        fixed * 16 + p * 4 + q,
                        p * 16 + fixed * 4 + q,
                        p * 16 + q * 4 + fixed,
                    )[face // 2]
                    select[face, a * 16 + p * 4 + q, a * 64 + n] = 1.0
    node_high, node_low = split_np(node)
    return (
        np.concatenate([node_high, node_high, node_low], axis=1),
        np.concatenate(split_np(fine), axis=0),
        np.concatenate(split_np(coarse), axis=0),
        select.reshape(480, 320).astype(ml_dtypes.bfloat16),
    )


def split(array):
    high = array.astype(BF16)
    return high, (array - high.astype(F32)).astype(BF16)


def mm(a, b):
    return jnp.dot(a, b, preferred_element_type=F32)


def side_by_side(high, low):
    return jnp.concatenate([high[:, :256], low[:, :256], high[:, 256:], low[:, 256:]], axis=1)


def product(a, b):
    high, low = split(b)
    blank = jnp.zeros_like(low)
    both = mm(
        a,
        jnp.concatenate(
            [
                jnp.concatenate([high[:256], high[:256], high[256:], high[256:]], axis=0),
                jnp.concatenate([low[:256], blank[:256], low[256:], blank[256:]], axis=0),
            ],
            axis=1,
        ),
    )
    n = b.shape[1]
    return both[:, :n] + both[:, n:]


def lanes(shape):
    return lax.broadcasted_iota(I32, shape, 1)


def rows(shape):
    return lax.broadcasted_iota(I32, shape, 0)


def stack_rows(parts, count):
    shape = (count, parts[0].shape[1])
    at = rows(shape)
    out = jnp.zeros(shape, F32)
    for i, part in enumerate(parts):
        out = jnp.where(at == i, part.astype(F32), out)
    return out


def onehot(index, shape):
    return jnp.where(index == rows(shape), 1.0, 0.0).astype(BF16)


def far_first(size):
    return sorted(range(size), key=lambda d: -min(d, size - d))


def outward(i, size):
    return lax.rem(size // 2 + (i + 1) // 2 * (1 - 2 * lax.rem(i, 2)) + size, size)


def kernel(
    n_gx,
    n_yz,
    hang,
    b_hbm,
    mass_hbm,
    coef_hbm,
    flux_hbm,
    first_hbm,
    final_hbm,
    mid_hbm,
    adj_hbm,
    plane_hbm,
    band_hbm,
    small_hbm,
    outq_hbm,
    incm_hbm,
    incq_hbm,
    cmts_hbm,
    node_hbm,
    fine_hbm,
    coarse_hbm,
    select_hbm,
    out_ref,
    b_ref,
    mass_ref,
    coef_ref,
    flux_ref,
    first_ref,
    final_ref,
    mid_ref,
    adj_ref,
    plane_ref,
    band_ref,
    small_ref,
    outq_ref,
    incm_ref,
    incq_ref,
    cmts_ref,
    node_ref,
    fine_ref,
    coarse_ref,
    select_ref,
    load_sem,
    x_ref,
    recv_ref,
    hx_ref,
    hrecv_ref,
    gx_ref,
    grecv_ref,
    px_ref,
    precv_ref,
    oh_ref,
    near_own_ref,
    near_in_ref,
    pick_ref,
    lift_ref,
    tr_ref,
    u_ref,
    send_sem,
    recv_sem,
):
    g, k = lax.axis_index("gx"), lax.axis_index("yz")
    wide = 8 * n_yz
    slots = CAP * n_yz
    barrier = pltpu.get_barrier_semaphore()

    n_y = 8 if n_yz % 16 == 0 else n_yz // 2
    n_x = n_yz // (2 * n_y)
    x, y, core = k // (2 * n_y), lax.rem(k // 2, n_y), lax.rem(k, 2)

    heights = [lax.rem(y + dy, n_y) * 2 for dy in far_first(n_y)]
    cores = (1 - core, core)

    def plane(act, start=0, end=n_y):
        def row(column, i, last):
            for j in range(start, end):
                for c in range(2):
                    if not (last and j == n_y - 1 and c == 1):
                        act(column + heights[j] + cores[c], (j * n_x + i) * 2 + c)

        def one(i, _):
            row(lax.rem(x + outward(i, n_x), n_x) * n_y * 2, i, False)
            return 0

        if n_x > 1:
            lax.fori_loop(0, n_x - 1, one, 0)
        row(x * n_y * 2, n_x - 1, True)

    mine = pl.ds(pl.multiple_of(8 * k, 8), 8)

    def greet(device, _):
        pl.semaphore_signal(barrier, inc=1, device_id=(g, device), device_id_type=MESH)

    plane(greet)
    gx_partners = [lax.rem(g + dg, n_gx) for dg in far_first(n_gx) if dg]
    for partner_g in gx_partners:
        pl.semaphore_signal(barrier, inc=1, device_id=(partner_g, k), device_id_type=MESH)
    loads = {}
    for i, (name, source, target) in enumerate(
        (
            ("first", first_hbm, first_ref),
            ("b", b_hbm, b_ref),
            ("small", small_hbm, small_ref),
            ("outq", outq_hbm, outq_ref),
            ("incm", incm_hbm, incm_ref),
            ("incq", incq_hbm, incq_ref),
            ("cmts", cmts_hbm, cmts_ref),
            ("plane", plane_hbm, plane_ref),
            ("band", band_hbm, band_ref),
            ("mid", mid_hbm, mid_ref),
            ("final", final_hbm, final_ref),
            ("select", select_hbm, select_ref),
            ("fine", fine_hbm, fine_ref),
            ("coarse", coarse_hbm, coarse_ref),
            ("node", node_hbm, node_ref),
            ("mass", mass_hbm, mass_ref),
            ("flux", flux_hbm, flux_ref),
            ("coef", coef_hbm, coef_ref),
            ("adj", adj_hbm, adj_ref),
        )
    ):
        loads[name] = pltpu.make_async_copy(source, target, load_sem.at[i])
        loads[name].start()

    def ready(*wanted):
        for name in wanted:
            loads[name].wait()

    half = n_yz // 2
    part = 8 * half
    place = lanes((1, 2 * part))
    place_c = lax.rem(place, part) // half
    place_i = (place // part) * half + lax.rem(place, half)
    jx = lax.rem(place_i, 2 * n_x) // 2
    place_x = jnp.zeros_like(jx)
    for j, dx in enumerate(far_first(n_x)):
        place_x = jnp.where(jx == j, dx, place_x)
    place_x = lax.rem(x + place_x, n_x)
    place_y = lax.rem(y + outward(place_i // (2 * n_x), n_y), n_y)
    place_core = lax.rem(core + 1 + place_i, 2)
    place_device = (place_x * n_y + place_y) * 2 + place_core

    ready("first", "b", "small", "outq", "incm", "incq", "cmts", "plane", "band")
    ready("mid", "final", "select", "fine", "coarse")
    first_high, first_low = split(first_ref[...])
    final_high, final_low = split(final_ref[...])
    first = side_by_side(first_high, first_low)
    final = side_by_side(final_high, final_low)
    select = select_ref[...]
    pick_ref[...] = mm(select, final).astype(BF16)

    mid = mid_ref[...]
    weighted = mid * product(first, b_ref[...])

    small = small_ref[...]
    incm = incm_ref[...]
    parts = [
        jnp.right_shift(small, 5),
        jnp.bitwise_and(small, 31),
        outq_ref[...],
        incm,
        incq_ref[...],
    ]
    live = place_c < CAP
    target = jnp.where(live, CAP * place_device + place_c, -1)
    spread = mm(stack_rows(parts, 16).astype(BF16), onehot(target, (slots, 2 * part)))
    spread = spread.astype(I32)
    fine_col = jnp.where(live, 32 * spread[0:1] + spread[1:2], -1)
    outq = spread[2:3]
    asked = jnp.where(live & (spread[3:4] < hang), spread[3:4], -1)
    incq = spread[4:5]
    cmts = cmts_ref[...]
    parts = [jnp.right_shift(cmts, 5), jnp.bitwise_and(cmts, 31)]
    found = mm(stack_rows(parts, 16).astype(BF16), onehot(asked, (hang, 2 * part))).astype(I32)
    coarse_col = jnp.where(asked >= 0, 32 * found[0:1] + found[1:2], -1)
    slab, side = plane_ref[0], band_ref[0]
    repeat = jnp.where(
        jnp.bitwise_and(lanes((HALO, 128)), HALO - 1) == rows((HALO, 128)), 1.0, 0.0
    ).astype(BF16)
    halo = mm(
        stack_rows([slab[0:1], slab[1:2], side[0:1], side[1:2]], 16).astype(BF16), repeat
    ).astype(I32)
    group = jnp.right_shift(lanes((1, 128)), 4)
    halo_col = jnp.full((1, 128), -1, I32)
    for i in range(4):
        halo_col = jnp.where(group == i, halo[i : i + 1] + 128 * i, halo_col)
    for i in range(2):
        cut = slice(part * i, part * i + part)
        at = 2 * part * i
        oh_ref[:, at : at + part] = onehot(fine_col[:, cut], (768, part))
        oh_ref[:, at + part : at + 2 * part] = onehot(coarse_col[:, cut], (768, part))
    oh_ref[:, 4 * part :] = onehot(halo_col, (768, 128))

    fine_w, coarse_w = fine_ref[...], coarse_ref[...]

    def masks(quadrant):
        return [jnp.where(quadrant == q, 1.0, 0.0).astype(BF16) for q in range(4)]

    out_masks, in_masks = masks(outq), masks(incq)

    def project(matrix, high, low, mask):
        def spread_out(values):
            values = values.astype(BF16)
            return jnp.concatenate([values * mask[q] for q in range(4)], axis=0)

        both = mm(matrix, spread_out(high))
        return both[:FACE] + both[FACE:] + mm(matrix[:FACE], spread_out(low))

    def send_part(step, i):
        cut = slice(part * i, part * i + part)
        gathered = mm(tr_ref[...], oh_ref[:, 2 * part * i : 2 * part * i + 2 * part])
        fine = project(
            fine_w, gathered[:FACE, :part], gathered[FACE:, :part], [m[:, cut] for m in out_masks]
        )
        coarse = project(
            coarse_w, gathered[:FACE, part:], gathered[FACE:, part:], [m[:, cut] for m in in_masks]
        )
        rest = [coarse[HEAD:, half * c : half * c + half] for c in range(CAP)]
        blank = jnp.zeros((32, half), F32)
        tails = jnp.concatenate(
            [
                jnp.concatenate([rest[j], rest[4 + j] if j < 2 else blank], axis=1)
                for j in range(4)
            ],
            axis=0,
        )
        head = jnp.concatenate([fine[:, : CAP * half], coarse[:HEAD, : CAP * half]], axis=0)
        packed = jnp.concatenate([head, tails], axis=1).T
        for c in range(8):
            x_ref[step, i, pl.ds(c, half, stride=8), :] = packed[
                half * c : half * c + half
            ]

    def start_part(step, i, start, end):
        def one(m, at):
            pltpu.make_async_remote_copy(
                src_ref=x_ref.at[step, i, pl.ds(pl.multiple_of(8 * at - part * i, 8), 8)],
                dst_ref=recv_ref.at[step, mine],
                send_sem=send_sem.at[step, 1],
                recv_sem=recv_sem.at[step, 1],
                device_id=(g, m),
                device_id_type=MESH,
            ).start()

        plane(one, start, end)

    def send(step, u_traces):
        high, low = split(u_traces)
        tr_ref[0:FACE] = jnp.concatenate(
            [high[FACE * f : FACE * (f + 1)] for f in range(6)], axis=1
        )
        tr_ref[FACE:] = jnp.concatenate([low[FACE * f : FACE * (f + 1)] for f in range(6)], axis=1)
        send_part(step, 0)
        if step == 0:
            pl.semaphore_wait(barrier, n_yz + n_gx - 2)
        start_part(step, 0, 0, n_y // 2)
        send_part(step, 1)
        start_part(step, 1, n_y // 2, n_y)
        halo_out = mm(tr_ref[...], oh_ref[:, 4 * part :])
        halo_out = halo_out[:FACE] + halo_out[FACE:]
        halo_out = jnp.concatenate([halo_out, jnp.zeros((48, 128), F32)], axis=0).T
        hx_ref[step] = halo_out[0 : 4 * HALO].reshape(4, HALO, 128)
        up_g, down_g = lax.rem(g + 1, n_gx), lax.rem(g + n_gx - 1, n_gx)
        up_k, down_k = lax.rem(k + 1, n_yz), lax.rem(k + n_yz - 1, n_yz)
        for source, target, device in (
            (0, 1, (down_g, k)),
            (1, 0, (up_g, k)),
            (2, 3, (g, down_k)),
            (3, 2, (g, up_k)),
        ):
            pltpu.make_async_remote_copy(
                src_ref=hx_ref.at[step, source],
                dst_ref=hrecv_ref.at[step, target],
                send_sem=send_sem.at[step, 0],
                recv_sem=recv_sem.at[step, 0],
                device_id=device,
                device_id_type=MESH,
            ).start()
        recv_ref[step, mine] = x_ref[step, 1, pl.ds(part - 8, 8)]

    def halo_copy(step):
        return pltpu.make_async_remote_copy(
            src_ref=hx_ref.at[step],
            dst_ref=hrecv_ref.at[step],
            send_sem=send_sem.at[step, 0],
            recv_sem=recv_sem.at[step, 0],
            device_id=(g, k),
            device_id_type=MESH,
        )

    def plane_copy(step):
        return pltpu.make_async_remote_copy(
            src_ref=recv_ref.at[step, pl.ds(0, wide - 8)],
            dst_ref=recv_ref.at[step, pl.ds(0, wide - 8)],
            send_sem=send_sem.at[step, 1],
            recv_sem=recv_sem.at[step, 1],
            device_id=(g, k),
            device_id_type=MESH,
        )

    def receive(step):
        halo_copy(step).wait_recv()
        plane_copy(step).wait_recv()
        tiles = jnp.concatenate(
            [recv_ref[step, pl.ds(c, n_yz, stride=8), :] for c in range(8)], axis=0
        ).T
        rest = jnp.concatenate(
            [
                tiles[
                    32 * (c % 4) : 32 * (c % 4) + 32,
                    n_yz * (CAP + c // 4) : n_yz * (CAP + c // 4) + n_yz,
                ]
                for c in range(CAP)
            ],
            axis=1,
        )
        halo_in = hrecv_ref[step].reshape(4 * HALO, 128)
        at = jnp.right_shift(rows((4 * HALO, 128)), 4)
        drop = ((at == 0) & (g == 0)) | ((at == 1) & (g == n_gx - 1))
        halo_in = jnp.where(drop, 0.0, halo_in)
        halo_in = jnp.concatenate([halo_in, jnp.zeros((64, 128), F32)], axis=0).T[:FACE]
        values = jnp.concatenate(
            [
                tiles[:FACE, :slots],
                jnp.concatenate([tiles[FACE:, :slots], rest], axis=0),
                halo_in,
            ],
            axis=1,
        )
        high, low = split(values)
        near = mm(jnp.concatenate([high, low], axis=0), near_in_ref[...])
        return near[:FACE] + near[FACE:]

    def volume(u):
        high, low = split(u)
        node = node_ref[...]

        def by_variable(part):
            return jnp.concatenate([part[64 * v : 64 * v + 64] for v in range(5)], axis=1)

        high, low = by_variable(high), by_variable(low)
        slopes = mm(node, jnp.concatenate([high, low, high], axis=0))
        out = []
        for a in range(5):
            total = mass_ref[64 * a : 64 * a + 64] * u[64 * a : 64 * a + 64]
            for d in range(3):
                for v in range(5):
                    row = d * 25 + a * 5 + v
                    total = (
                        total
                        + flux_ref[row : row + 1]
                        * slopes[64 * d : 64 * d + 64, 128 * v : 128 * v + 128]
                    )
            out.append(total)
        return product(first, jnp.concatenate(out, axis=0))

    def own_near():
        near = mm(tr_ref[...], near_own_ref[...])
        return near[:FACE] + near[FACE:]

    def lifted(jumps):
        high, low = split(jumps)
        both = mm(lift_ref[0], jnp.concatenate([high, low], axis=1))
        return both[:, :128] + both[:, 128:] + mm(lift_ref[1], high)

    def finish(base, traces, near_own, near_in):
        near = near_own + near_in
        jumps = jnp.concatenate(
            [
                coef_ref[FACE * f : FACE * (f + 1)]
                * (traces[FACE * f : FACE * (f + 1)] - near[:, 128 * f : 128 * f + 128])
                for f in range(6)
            ],
            axis=0,
        )
        return (mid * SCALE) * (base + lifted(jumps))

    def fold(a, b):
        return jnp.sum(a * b, axis=0, keepdims=True)

    traces = product(pick_ref[...], weighted)
    send(0, traces)
    u_ref[0] = product(final, weighted)
    nt = (((1,), (1,)), ((), ()))
    lift_ref[0] = lax.dot_general(
        first_high, select, nt, preferred_element_type=F32
    ).astype(BF16)
    lift_ref[1] = lax.dot_general(
        first_low, select, nt, preferred_element_type=F32
    ).astype(BF16)
    ready("node", "mass", "flux", "coef", "adj")
    table = 768 + 4 * HALO
    lane = lanes((1, slots))
    natural = CAP * lax.rem(lane, n_yz) + lane // n_yz
    owned = mm(stack_rows([incm], 16).astype(BF16), onehot(natural, (slots, slots)))[0:1]
    owned = owned.astype(I32)
    owned = jnp.where(owned < hang, owned + table, -1)
    owned_col = jnp.broadcast_to(owned, (128, slots)).T
    slot = rows((slots, 128))
    reply = CAP * lax.rem(slot, n_yz) + slot // n_yz + table + hang
    halo_at = rows((128, 128))
    halo_at = jnp.where(halo_at < 4 * HALO, halo_at + 768, -1)
    for f in range(6):
        adj = adj_ref[f : f + 1]
        near_own_ref[:, 128 * f : 128 * f + 128] = onehot(adj, (768, 128))
        near_in_ref[0:slots, 128 * f : 128 * f + 128] = jnp.where(
            owned_col == adj, 1.0, 0.0
        ).astype(BF16)
        near_in_ref[slots : 2 * slots, 128 * f : 128 * f + 128] = jnp.where(
            reply == adj, 1.0, 0.0
        ).astype(BF16)
        near_in_ref[2 * slots :, 128 * f : 128 * f + 128] = jnp.where(
            halo_at == adj, 1.0, 0.0
        ).astype(BF16)
    base = volume(u_ref[0])
    near_own = own_near()
    weighted = finish(base, traces, near_own, receive(0))

    traces = product(pick_ref[...], weighted)
    send(1, traces)
    u_ref[1] = product(final, weighted)
    base = volume(u_ref[1])
    near_own = own_near()
    r, u1 = u_ref[0], u_ref[1]
    g00, g01, g11 = fold(r, r), fold(r, u1), fold(u1, u1)
    weighted = finish(base, traces, near_own, receive(1))
    u2 = product(final, weighted)

    gram = stack_rows([g00, g01, g11, fold(r, u2), fold(u1, u2), fold(u2, u2)], 8)
    column = jnp.sum(gram, axis=1, keepdims=True)
    gram = jnp.where(rows((8, 128)) == lanes((8, 128)), column, 0.0)
    gram = jnp.sum(gram, axis=0, keepdims=True)
    px_ref[...] = gram

    def one(m, _):
        pltpu.make_async_remote_copy(
            src_ref=px_ref,
            dst_ref=precv_ref.at[k],
            send_sem=send_sem.at[2, 1],
            recv_sem=recv_sem.at[2, 1],
            device_id=(g, m),
            device_id_type=MESH,
        ).start()

    plane(one)
    precv_ref[pl.ds(k, 1)] = gram.reshape(1, 1, 128)
    sum_copy = pltpu.make_async_remote_copy(
        src_ref=precv_ref.at[pl.ds(0, n_yz - 1)],
        dst_ref=precv_ref.at[pl.ds(0, n_yz - 1)],
        send_sem=send_sem.at[2, 1],
        recv_sem=recv_sem.at[2, 1],
        device_id=(g, k),
        device_id_type=MESH,
    )
    sum_copy.wait_recv()
    gram = jnp.sum(precv_ref[...], axis=0)
    gx_ref[...] = gram
    for partner_g in gx_partners:
        pltpu.make_async_remote_copy(
            src_ref=gx_ref,
            dst_ref=grecv_ref.at[g],
            send_sem=send_sem.at[2, 0],
            recv_sem=recv_sem.at[2, 0],
            device_id=(partner_g, k),
            device_id_type=MESH,
        ).start()
    grecv_ref[pl.ds(g, 1)] = gram.reshape(1, 1, 128)
    gram_copy = pltpu.make_async_remote_copy(
        src_ref=grecv_ref.at[pl.ds(0, n_gx - 1)],
        dst_ref=grecv_ref.at[pl.ds(0, n_gx - 1)],
        send_sem=send_sem.at[2, 0],
        recv_sem=recv_sem.at[2, 0],
        device_id=(g, k),
        device_id_type=MESH,
    )
    gram_copy.wait_recv()
    total = jnp.sum(grecv_ref[...], axis=0)
    at = lanes((1, 128))

    def entry(i):
        return jnp.sum(jnp.where(at == i, total, 0.0), axis=1, keepdims=True)

    c_r, c_u = coefficients(*[entry(i) for i in range(6)])
    out_ref[...] = c_r * u_ref[0] + c_u * u_ref[1]

    for step in range(2):
        halo_copy(step).wait_send()
        plane_copy(step).wait_send()
    gram_copy.wait_send()
    sum_copy.wait_send()


def coefficients(g00, g01, g11, g02, g12, g22):
    s = SCALE
    beta = jnp.sqrt(g00 + EPSILON)
    h00 = g01 / (s * beta * beta)
    p1, p0 = 1.0 / s, -h00
    norm = (p1 * p1 * g11 + 2.0 * p1 * p0 * g01 + p0 * p0 * g00) / (beta * beta)
    h10 = jnp.sqrt(jnp.maximum(norm, 0.0) + EPSILON)
    c1, c0 = p1 / (beta * h10), p0 / (beta * h10)
    a2, a1 = c1 / s, c0 / s
    h01 = (a2 * g02 + a1 * g01) / beta
    a0 = -h01 / beta
    h11 = c1 * (a2 * g12 + a1 * g11 + a0 * g01) + c0 * (a2 * g02 + a1 * g01 + a0 * g00)
    a1, a0 = a1 - h11 * c1, a0 - h11 * c0
    norm = a2 * (a2 * g22 + 2.0 * (a1 * g12 + a0 * g02)) + (
        a1 * (a1 * g11 + 2.0 * a0 * g01) + a0 * a0 * g00
    )
    h21 = jnp.sqrt(jnp.maximum(norm, 0.0) + EPSILON)
    radius = jnp.sqrt(h00 * h00 + h10 * h10)
    cos0, sin0 = h00 / radius, h10 / radius
    top = cos0 * h01 + sin0 * h11
    low = cos0 * h11 - sin0 * h01
    length = jnp.sqrt(low * low + h21 * h21)
    y1 = (low / length) * (-sin0 * beta) / length
    y0 = (cos0 * beta - top * y1) / radius
    return y0 / beta + y1 * c0, y1 * c1


def on_device(
    n_gx,
    n_yz,
    source,
    mass,
    coupling,
    flux,
    first,
    final,
    middle,
    adjacent,
    plane,
    band,
    small,
    proprietor,
    outq,
    incm,
    incq,
    cmts,
):
    del proprietor
    tables = [jnp.asarray(t) for t in gll_tables()]
    wide, slots = 8 * n_yz, CAP * n_yz
    arguments = (
        source, mass, coupling, flux, first, final, middle, adjacent, plane, band,
        small, outq, incm, incq, cmts, *tables,
    )
    vmem = pl.BlockSpec(memory_space=pltpu.VMEM)
    hbm = pl.BlockSpec(memory_space=pltpu.HBM)
    return pl.pallas_call(
        functools.partial(kernel, n_gx, n_yz, cmts.shape[1]),
        out_shape=jax.ShapeDtypeStruct(source.shape, F32),
        in_specs=[hbm] * len(arguments),
        out_specs=vmem,
        scratch_shapes=[
            *[pltpu.VMEM(a.shape, a.dtype) for a in arguments],
            pltpu.SemaphoreType.DMA((len(arguments),)),
            pltpu.VMEM((2, 2, wide // 2, 128), F32),
            pltpu.VMEM((2, wide, 128), F32),
            pltpu.VMEM((2, 4, HALO, 128), F32),
            pltpu.VMEM((2, 4, HALO, 128), F32),
            pltpu.VMEM((1, 128), F32),
            pltpu.VMEM((n_gx, 1, 128), F32),
            pltpu.VMEM((1, 128), F32),
            pltpu.VMEM((n_yz, 1, 128), F32),
            pltpu.VMEM((768, 4 * wide // 2 + 128), BF16),
            pltpu.VMEM((768, 768), BF16),
            pltpu.VMEM((2 * slots + 128, 768), BF16),
            pltpu.VMEM((480, 640), BF16),
            pltpu.VMEM((2, 320, 480), BF16),
            pltpu.VMEM((2 * FACE, 768), BF16),
            pltpu.VMEM((2, 320, 128), F32),
            pltpu.SemaphoreType.DMA((3, 2)),
            pltpu.SemaphoreType.DMA((3, 2)),
        ],
        compiler_params=pltpu.CompilerParams(
            collective_id=0, has_side_effects=True, vmem_limit_bytes=63 * 1024 * 1024
        ),
    )(*arguments)


def solution(mesh):
    n_gx, n_yz = mesh.shape["gx"], mesh.shape["yz"]
    both = ("gx", "yz")
    field, lists = P(None, both), P(both, None)
    return jax.shard_map(
        functools.partial(on_device, n_gx, n_yz),
        mesh=mesh,
        in_specs=(
            field, field, field, field, P(), P(), field, field,
            P(both, None, None), P(both, None, None),
            lists, lists, lists, lists, lists, lists,
        ),
        out_specs=field,
        check_vma=False,
    )
```

```python
import functools

import jax
import jax.numpy as jnp
import ml_dtypes
import numpy as np
from jax import lax
from jax.experimental import pallas as pl
from jax.experimental.pallas import tpu as pltpu
from jax.sharding import PartitionSpec as P

MESH = pl.DeviceIdType.MESH
F32 = jnp.float32
BF16 = jnp.bfloat16
I32 = jnp.int32

EPSILON = 1e-6
SCALE = 2.0**-10
CAP = 6
FACE = 80
HALO = 16
HEAD = 128 - FACE


def split_np(array):
    high = array.astype(np.float32).astype(ml_dtypes.bfloat16)
    low = (array - high.astype(np.float64)).astype(np.float32).astype(ml_dtypes.bfloat16)
    return high, low


def gll_tables():
    inv_root = 1.0 / np.sqrt(5.0)
    points = np.array([-1.0, -inv_root, inv_root, 1.0])
    weights = np.array([1.0, 5.0, 5.0, 1.0]) / 6.0

    def lagrange(at):
        values = np.ones((len(at), 4))
        for j in range(4):
            for m in range(4):
                if m != j:
                    values[:, j] = values[:, j] * (at - points[m]) / (points[j] - points[m])
        return values

    derivative = np.zeros((4, 4))
    for i in range(4):
        for j in range(4):
            for m in range(4):
                if m != j:
                    term = 1.0 / (points[j] - points[m])
                    for n in range(4):
                        if n != j and n != m:
                            term = term * (points[i] - points[n]) / (points[j] - points[n])
                    derivative[i, j] += term
    halves = [lagrange((points - 1.0) / 2.0), lagrange((points + 1.0) / 2.0)]
    projections = [0.5 * (1.0 / weights)[:, None] * h.T * weights[None, :] for h in halves]
    one5, one4 = np.eye(5), np.eye(4)
    fine = np.concatenate(
        [np.kron(one5, np.kron(projections[q // 2], projections[q % 2])) for q in range(4)], axis=1
    )
    coarse = np.concatenate(
        [np.kron(one5, np.kron(halves[q // 2], halves[q % 2])) for q in range(4)], axis=1
    )
    node = np.concatenate(
        [
            np.kron(derivative, np.kron(one4, one4)),
            np.kron(one4, np.kron(derivative, one4)),
            np.kron(one4, np.kron(one4, derivative)),
        ],
        axis=0,
    )
    select = np.zeros((6, FACE, 320))
    for face in range(6):
        fixed = 3 * (face % 2)
        for a in range(5):
            for p in range(4):
                for q in range(4):
                    n = (
                        fixed * 16 + p * 4 + q,
                        p * 16 + fixed * 4 + q,
                        p * 16 + q * 4 + fixed,
                    )[face // 2]
                    select[face, a * 16 + p * 4 + q, a * 64 + n] = 1.0
    node_high, node_low = split_np(node)
    return (
        np.concatenate([node_high, node_high, node_low], axis=1),
        np.concatenate(split_np(fine), axis=0),
        np.concatenate(split_np(coarse), axis=0),
        select.reshape(480, 320).astype(ml_dtypes.bfloat16),
    )


def split(array):
    high = array.astype(BF16)
    return high, (array - high.astype(F32)).astype(BF16)


def mm(a, b):
    return jnp.dot(a, b, preferred_element_type=F32)


def side_by_side(high, low):
    return jnp.concatenate([high[:, :256], low[:, :256], high[:, 256:], low[:, 256:]], axis=1)


def product(a, b):
    high, low = split(b)
    blank = jnp.zeros_like(low)
    both = mm(
        a,
        jnp.concatenate(
            [
                jnp.concatenate([high[:256], high[:256], high[256:], high[256:]], axis=0),
                jnp.concatenate([low[:256], blank[:256], low[256:], blank[256:]], axis=0),
            ],
            axis=1,
        ),
    )
    n = b.shape[1]
    return both[:, :n] + both[:, n:]


def lanes(shape):
    return lax.broadcasted_iota(I32, shape, 1)


def rows(shape):
    return lax.broadcasted_iota(I32, shape, 0)


def stack_rows(parts, count):
    shape = (count, parts[0].shape[1])
    at = rows(shape)
    out = jnp.zeros(shape, F32)
    for i, part in enumerate(parts):
        out = jnp.where(at == i, part.astype(F32), out)
    return out


def onehot(index, shape):
    return jnp.where(index == rows(shape), 1.0, 0.0).astype(BF16)


def far_first(size):
    return sorted(range(size), key=lambda d: -min(d, size - d))


def outward(i, size):
    return lax.rem(size // 2 + (i + 1) // 2 * (1 - 2 * lax.rem(i, 2)) + size, size)


def kernel(
    n_gx,
    n_yz,
    hang,
    b_hbm,
    mass_hbm,
    coef_hbm,
    flux_hbm,
    first_hbm,
    final_hbm,
    mid_hbm,
    adj_hbm,
    plane_hbm,
    band_hbm,
    small_hbm,
    outq_hbm,
    incm_hbm,
    incq_hbm,
    cmts_hbm,
    node_hbm,
    fine_hbm,
    coarse_hbm,
    select_hbm,
    out_hbm,
    out_ref,
    b_ref,
    mass_ref,
    coef_ref,
    flux_ref,
    first_ref,
    final_ref,
    mid_ref,
    adj_ref,
    plane_ref,
    band_ref,
    small_ref,
    outq_ref,
    incm_ref,
    incq_ref,
    cmts_ref,
    node_ref,
    fine_ref,
    coarse_ref,
    select_ref,
    load_sem,
    x_ref,
    recv_ref,
    hx_ref,
    hrecv_ref,
    gx_ref,
    grecv_ref,
    px_ref,
    precv_ref,
    oh_ref,
    near_own_ref,
    near_in_ref,
    pick_ref,
    lift_ref,
    tr_ref,
    u_ref,
    send_sem,
    recv_sem,
    store_sem,
):
    g, k = lax.axis_index("gx"), lax.axis_index("yz")
    wide = 8 * n_yz
    slots = CAP * n_yz
    barrier = pltpu.get_barrier_semaphore()

    n_y = 8 if n_yz % 16 == 0 else n_yz // 2
    n_x = n_yz // (2 * n_y)
    x, y, core = k // (2 * n_y), lax.rem(k // 2, n_y), lax.rem(k, 2)

    heights = [lax.rem(y + dy, n_y) * 2 for dy in far_first(n_y)]
    cores = (1 - core, core)

    def plane(act, start=0, end=n_y):
        def row(column, i, last):
            for j in range(start, end):
                for c in range(2):
                    if not (last and j == n_y - 1 and c == 1):
                        act(column + heights[j] + cores[c], (j * n_x + i) * 2 + c)

        def one(i, _):
            row(lax.rem(x + outward(i, n_x), n_x) * n_y * 2, i, False)
            return 0

        if n_x > 1:
            lax.fori_loop(0, n_x - 1, one, 0)
        row(x * n_y * 2, n_x - 1, True)

    mine = pl.ds(pl.multiple_of(8 * k, 8), 8)

    def greet(device, _):
        pl.semaphore_signal(barrier, inc=1, device_id=(g, device), device_id_type=MESH)

    plane(greet)
    gx_partners = [lax.rem(g + dg, n_gx) for dg in far_first(n_gx) if dg]
    for partner_g in gx_partners:
        pl.semaphore_signal(barrier, inc=1, device_id=(partner_g, k), device_id_type=MESH)
    loads = {}
    for i, (name, source, target) in enumerate(
        (
            ("first", first_hbm, first_ref),
            ("b", b_hbm, b_ref),
            ("small", small_hbm, small_ref),
            ("outq", outq_hbm, outq_ref),
            ("incm", incm_hbm, incm_ref),
            ("incq", incq_hbm, incq_ref),
            ("cmts", cmts_hbm, cmts_ref),
            ("plane", plane_hbm, plane_ref),
            ("band", band_hbm, band_ref),
            ("mid", mid_hbm, mid_ref),
            ("final", final_hbm, final_ref),
            ("select", select_hbm, select_ref),
            ("fine", fine_hbm, fine_ref),
            ("coarse", coarse_hbm, coarse_ref),
            ("node", node_hbm, node_ref),
            ("mass", mass_hbm, mass_ref),
            ("flux", flux_hbm, flux_ref),
            ("coef", coef_hbm, coef_ref),
            ("adj", adj_hbm, adj_ref),
        )
    ):
        loads[name] = pltpu.make_async_copy(source, target, load_sem.at[i])
        loads[name].start()

    def ready(*wanted):
        for name in wanted:
            loads[name].wait()

    half = n_yz // 2
    part = 8 * half
    place = lanes((1, 2 * part))
    place_c = lax.rem(place, part) // half
    place_i = (place // part) * half + lax.rem(place, half)
    jx = lax.rem(place_i, 2 * n_x) // 2
    place_x = jnp.zeros_like(jx)
    for j, dx in enumerate(far_first(n_x)):
        place_x = jnp.where(jx == j, dx, place_x)
    place_x = lax.rem(x + place_x, n_x)
    place_y = lax.rem(y + outward(place_i // (2 * n_x), n_y), n_y)
    place_core = lax.rem(core + 1 + place_i, 2)
    place_device = (place_x * n_y + place_y) * 2 + place_core

    ready("first", "b", "small", "outq", "incm", "incq", "cmts", "plane", "band")
    ready("mid", "final", "select", "fine", "coarse")
    first_high, first_low = split(first_ref[...])
    final_high, final_low = split(final_ref[...])
    first = side_by_side(first_high, first_low)
    final = side_by_side(final_high, final_low)
    select = select_ref[...]
    pick_ref[...] = mm(select, final).astype(BF16)

    mid = mid_ref[...]
    weighted = mid * product(first, b_ref[...])

    small = small_ref[...]
    incm = incm_ref[...]
    parts = [
        jnp.right_shift(small, 5),
        jnp.bitwise_and(small, 31),
        outq_ref[...],
        incm,
        incq_ref[...],
    ]
    live = place_c < CAP
    target = jnp.where(live, CAP * place_device + place_c, -1)
    spread = mm(stack_rows(parts, 16).astype(BF16), onehot(target, (slots, 2 * part)))
    spread = spread.astype(I32)
    fine_col = jnp.where(live, 32 * spread[0:1] + spread[1:2], -1)
    outq = spread[2:3]
    asked = jnp.where(live & (spread[3:4] < hang), spread[3:4], -1)
    incq = spread[4:5]
    cmts = cmts_ref[...]
    parts = [jnp.right_shift(cmts, 5), jnp.bitwise_and(cmts, 31)]
    found = mm(stack_rows(parts, 16).astype(BF16), onehot(asked, (hang, 2 * part))).astype(I32)
    coarse_col = jnp.where(asked >= 0, 32 * found[0:1] + found[1:2], -1)
    slab, side = plane_ref[0], band_ref[0]
    repeat = jnp.where(
        jnp.bitwise_and(lanes((HALO, 128)), HALO - 1) == rows((HALO, 128)), 1.0, 0.0
    ).astype(BF16)
    halo = mm(
        stack_rows([slab[0:1], slab[1:2], side[0:1], side[1:2]], 16).astype(BF16), repeat
    ).astype(I32)
    group = jnp.right_shift(lanes((1, 128)), 4)
    halo_col = jnp.full((1, 128), -1, I32)
    for i in range(4):
        halo_col = jnp.where(group == i, halo[i : i + 1] + 128 * i, halo_col)
    for i in range(2):
        cut = slice(part * i, part * i + part)
        at = 2 * part * i
        oh_ref[:, at : at + part] = onehot(fine_col[:, cut], (768, part))
        oh_ref[:, at + part : at + 2 * part] = onehot(coarse_col[:, cut], (768, part))
    oh_ref[:, 4 * part :] = onehot(halo_col, (768, 128))

    fine_w, coarse_w = fine_ref[...], coarse_ref[...]

    def masks(quadrant):
        return [jnp.where(quadrant == q, 1.0, 0.0).astype(BF16) for q in range(4)]

    out_masks, in_masks = masks(outq), masks(incq)

    def project(matrix, high, low, mask):
        def spread_out(values):
            values = values.astype(BF16)
            return jnp.concatenate([values * mask[q] for q in range(4)], axis=0)

        both = mm(matrix, spread_out(high))
        return both[:FACE] + both[FACE:] + mm(matrix[:FACE], spread_out(low))

    def send_part(step, i):
        cut = slice(part * i, part * i + part)
        gathered = mm(tr_ref[...], oh_ref[:, 2 * part * i : 2 * part * i + 2 * part])
        fine = project(
            fine_w, gathered[:FACE, :part], gathered[FACE:, :part], [m[:, cut] for m in out_masks]
        )
        coarse = project(
            coarse_w, gathered[:FACE, part:], gathered[FACE:, part:], [m[:, cut] for m in in_masks]
        )
        rest = [coarse[HEAD:, half * c : half * c + half] for c in range(CAP)]
        blank = jnp.zeros((32, half), F32)
        tails = jnp.concatenate(
            [
                jnp.concatenate([rest[j], rest[4 + j] if j < 2 else blank], axis=1)
                for j in range(4)
            ],
            axis=0,
        )
        head = jnp.concatenate([fine[:, : CAP * half], coarse[:HEAD, : CAP * half]], axis=0)
        packed = jnp.concatenate([head, tails], axis=1).T
        for c in range(8):
            x_ref[step, i, pl.ds(c, half, stride=8), :] = packed[
                half * c : half * c + half
            ]

    def start_part(step, i, start, end):
        def one(m, at):
            pltpu.make_async_remote_copy(
                src_ref=x_ref.at[step, i, pl.ds(pl.multiple_of(8 * at - part * i, 8), 8)],
                dst_ref=recv_ref.at[step, mine],
                send_sem=send_sem.at[step, 1],
                recv_sem=recv_sem.at[step, 1],
                device_id=(g, m),
                device_id_type=MESH,
            ).start()

        plane(one, start, end)

    def send(step, u_traces):
        high, low = split(u_traces)
        tr_ref[0:FACE] = jnp.concatenate(
            [high[FACE * f : FACE * (f + 1)] for f in range(6)], axis=1
        )
        tr_ref[FACE:] = jnp.concatenate([low[FACE * f : FACE * (f + 1)] for f in range(6)], axis=1)
        send_part(step, 0)
        if step == 0:
            pl.semaphore_wait(barrier, n_yz + n_gx - 2)
        start_part(step, 0, 0, n_y // 2)
        send_part(step, 1)
        start_part(step, 1, n_y // 2, n_y)
        halo_out = mm(tr_ref[...], oh_ref[:, 4 * part :])
        halo_out = halo_out[:FACE] + halo_out[FACE:]
        halo_out = jnp.concatenate([halo_out, jnp.zeros((48, 128), F32)], axis=0).T
        hx_ref[step] = halo_out[0 : 4 * HALO].reshape(4, HALO, 128)
        up_g, down_g = lax.rem(g + 1, n_gx), lax.rem(g + n_gx - 1, n_gx)
        up_k, down_k = lax.rem(k + 1, n_yz), lax.rem(k + n_yz - 1, n_yz)
        for source, target, device in (
            (0, 1, (down_g, k)),
            (1, 0, (up_g, k)),
            (2, 3, (g, down_k)),
            (3, 2, (g, up_k)),
        ):
            pltpu.make_async_remote_copy(
                src_ref=hx_ref.at[step, source],
                dst_ref=hrecv_ref.at[step, target],
                send_sem=send_sem.at[step, 0],
                recv_sem=recv_sem.at[step, 0],
                device_id=device,
                device_id_type=MESH,
            ).start()
        recv_ref[step, mine] = x_ref[step, 1, pl.ds(part - 8, 8)]

    def halo_copy(step):
        return pltpu.make_async_remote_copy(
            src_ref=hx_ref.at[step],
            dst_ref=hrecv_ref.at[step],
            send_sem=send_sem.at[step, 0],
            recv_sem=recv_sem.at[step, 0],
            device_id=(g, k),
            device_id_type=MESH,
        )

    def plane_copy(step):
        return pltpu.make_async_remote_copy(
            src_ref=recv_ref.at[step, pl.ds(0, wide - 8)],
            dst_ref=recv_ref.at[step, pl.ds(0, wide - 8)],
            send_sem=send_sem.at[step, 1],
            recv_sem=recv_sem.at[step, 1],
            device_id=(g, k),
            device_id_type=MESH,
        )

    def receive(step):
        halo_copy(step).wait_recv()
        plane_copy(step).wait_recv()
        tiles = jnp.concatenate(
            [recv_ref[step, pl.ds(c, n_yz, stride=8), :] for c in range(8)], axis=0
        ).T
        rest = jnp.concatenate(
            [
                tiles[
                    32 * (c % 4) : 32 * (c % 4) + 32,
                    n_yz * (CAP + c // 4) : n_yz * (CAP + c // 4) + n_yz,
                ]
                for c in range(CAP)
            ],
            axis=1,
        )
        halo_in = hrecv_ref[step].reshape(4 * HALO, 128)
        at = jnp.right_shift(rows((4 * HALO, 128)), 4)
        drop = ((at == 0) & (g == 0)) | ((at == 1) & (g == n_gx - 1))
        halo_in = jnp.where(drop, 0.0, halo_in)
        halo_in = jnp.concatenate([halo_in, jnp.zeros((64, 128), F32)], axis=0).T[:FACE]
        values = jnp.concatenate(
            [
                tiles[:FACE, :slots],
                jnp.concatenate([tiles[FACE:, :slots], rest], axis=0),
                halo_in,
            ],
            axis=1,
        )
        high, low = split(values)
        near = mm(jnp.concatenate([high, low], axis=0), near_in_ref[...])
        return near[:FACE] + near[FACE:]

    def volume(u):
        high, low = split(u)
        node = node_ref[...]

        def by_variable(part):
            return jnp.concatenate([part[64 * v : 64 * v + 64] for v in range(5)], axis=1)

        high, low = by_variable(high), by_variable(low)
        slopes = mm(node, jnp.concatenate([high, low, high], axis=0))
        out = []
        for a in range(5):
            total = mass_ref[64 * a : 64 * a + 64] * u[64 * a : 64 * a + 64]
            for d in range(3):
                for v in range(5):
                    row = d * 25 + a * 5 + v
                    total = (
                        total
                        + flux_ref[row : row + 1]
                        * slopes[64 * d : 64 * d + 64, 128 * v : 128 * v + 128]
                    )
            out.append(total)
        return product(first, jnp.concatenate(out, axis=0))

    def own_near():
        near = mm(tr_ref[...], near_own_ref[...])
        return near[:FACE] + near[FACE:]

    def lifted(jumps):
        high, low = split(jumps)
        both = mm(lift_ref[0], jnp.concatenate([high, low], axis=1))
        return both[:, :128] + both[:, 128:] + mm(lift_ref[1], high)

    def finish(base, traces, near_own, near_in):
        near = near_own + near_in
        jumps = jnp.concatenate(
            [
                coef_ref[FACE * f : FACE * (f + 1)]
                * (traces[FACE * f : FACE * (f + 1)] - near[:, 128 * f : 128 * f + 128])
                for f in range(6)
            ],
            axis=0,
        )
        return (mid * SCALE) * (base + lifted(jumps))

    def fold(a, b):
        return jnp.sum(a * b, axis=0, keepdims=True)

    traces = product(pick_ref[...], weighted)
    send(0, traces)
    u_ref[0] = product(final, weighted)
    nt = (((1,), (1,)), ((), ()))
    lift_ref[0] = lax.dot_general(
        first_high, select, nt, preferred_element_type=F32
    ).astype(BF16)
    lift_ref[1] = lax.dot_general(
        first_low, select, nt, preferred_element_type=F32
    ).astype(BF16)
    ready("node", "mass", "flux", "coef", "adj")
    table = 768 + 4 * HALO
    lane = lanes((1, slots))
    natural = CAP * lax.rem(lane, n_yz) + lane // n_yz
    owned = mm(stack_rows([incm], 16).astype(BF16), onehot(natural, (slots, slots)))[0:1]
    owned = owned.astype(I32)
    owned = jnp.where(owned < hang, owned + table, -1)
    owned_col = jnp.broadcast_to(owned, (128, slots)).T
    slot = rows((slots, 128))
    reply = CAP * lax.rem(slot, n_yz) + slot // n_yz + table + hang
    halo_at = rows((128, 128))
    halo_at = jnp.where(halo_at < 4 * HALO, halo_at + 768, -1)
    for f in range(6):
        adj = adj_ref[f : f + 1]
        near_own_ref[:, 128 * f : 128 * f + 128] = onehot(adj, (768, 128))
        near_in_ref[0:slots, 128 * f : 128 * f + 128] = jnp.where(
            owned_col == adj, 1.0, 0.0
        ).astype(BF16)
        near_in_ref[slots : 2 * slots, 128 * f : 128 * f + 128] = jnp.where(
            reply == adj, 1.0, 0.0
        ).astype(BF16)
        near_in_ref[2 * slots :, 128 * f : 128 * f + 128] = jnp.where(
            halo_at == adj, 1.0, 0.0
        ).astype(BF16)
    base = volume(u_ref[0])
    near_own = own_near()
    weighted = finish(base, traces, near_own, receive(0))

    traces = product(pick_ref[...], weighted)
    send(1, traces)
    u_ref[1] = product(final, weighted)
    base = volume(u_ref[1])
    near_own = own_near()
    r, u1 = u_ref[0], u_ref[1]
    g00, g01, g11 = fold(r, r), fold(r, u1), fold(u1, u1)
    weighted = finish(base, traces, near_own, receive(1))
    u2 = product(final, weighted)

    gram = stack_rows([g00, g01, g11, fold(r, u2), fold(u1, u2), fold(u2, u2)], 8)
    column = jnp.sum(gram, axis=1, keepdims=True)
    gram = jnp.where(rows((8, 128)) == lanes((8, 128)), column, 0.0)
    gram = jnp.sum(gram, axis=0, keepdims=True)
    px_ref[...] = gram

    def one(m, _):
        pltpu.make_async_remote_copy(
            src_ref=px_ref,
            dst_ref=precv_ref.at[k],
            send_sem=send_sem.at[2, 1],
            recv_sem=recv_sem.at[2, 1],
            device_id=(g, m),
            device_id_type=MESH,
        ).start()

    plane(one)
    precv_ref[pl.ds(k, 1)] = gram.reshape(1, 1, 128)
    sum_copy = pltpu.make_async_remote_copy(
        src_ref=precv_ref.at[pl.ds(0, n_yz - 1)],
        dst_ref=precv_ref.at[pl.ds(0, n_yz - 1)],
        send_sem=send_sem.at[2, 1],
        recv_sem=recv_sem.at[2, 1],
        device_id=(g, k),
        device_id_type=MESH,
    )
    sum_copy.wait_recv()
    gram = jnp.sum(precv_ref[...], axis=0)
    gx_ref[...] = gram
    for partner_g in gx_partners:
        pltpu.make_async_remote_copy(
            src_ref=gx_ref,
            dst_ref=grecv_ref.at[g],
            send_sem=send_sem.at[2, 0],
            recv_sem=recv_sem.at[2, 0],
            device_id=(partner_g, k),
            device_id_type=MESH,
        ).start()
    grecv_ref[pl.ds(g, 1)] = gram.reshape(1, 1, 128)
    gram_copy = pltpu.make_async_remote_copy(
        src_ref=grecv_ref.at[pl.ds(0, n_gx - 1)],
        dst_ref=grecv_ref.at[pl.ds(0, n_gx - 1)],
        send_sem=send_sem.at[2, 0],
        recv_sem=recv_sem.at[2, 0],
        device_id=(g, k),
        device_id_type=MESH,
    )
    gram_copy.wait_recv()
    total = jnp.sum(grecv_ref[...], axis=0)
    at = lanes((1, 128))

    def entry(i):
        return jnp.sum(jnp.where(at == i, total, 0.0), axis=1, keepdims=True)

    c_r, c_u = coefficients(*[entry(i) for i in range(6)])
    stores = []
    for i in range(2):
        at = pl.ds(160 * i, 160)
        out_ref[at] = c_r * u_ref[0, at] + c_u * u_ref[1, at]
        stores.append(pltpu.make_async_copy(out_ref.at[at], out_hbm.at[at], store_sem.at[i]))
        stores[i].start()

    for step in range(2):
        halo_copy(step).wait_send()
        plane_copy(step).wait_send()
    gram_copy.wait_send()
    sum_copy.wait_send()
    for store in stores:
        store.wait()


def coefficients(g00, g01, g11, g02, g12, g22):
    s = SCALE
    beta = jnp.sqrt(g00 + EPSILON)
    h00 = g01 / (s * beta * beta)
    p1, p0 = 1.0 / s, -h00
    norm = (p1 * p1 * g11 + 2.0 * p1 * p0 * g01 + p0 * p0 * g00) / (beta * beta)
    h10 = jnp.sqrt(jnp.maximum(norm, 0.0) + EPSILON)
    c1, c0 = p1 / (beta * h10), p0 / (beta * h10)
    a2, a1 = c1 / s, c0 / s
    h01 = (a2 * g02 + a1 * g01) / beta
    a0 = -h01 / beta
    h11 = c1 * (a2 * g12 + a1 * g11 + a0 * g01) + c0 * (a2 * g02 + a1 * g01 + a0 * g00)
    a1, a0 = a1 - h11 * c1, a0 - h11 * c0
    norm = a2 * (a2 * g22 + 2.0 * (a1 * g12 + a0 * g02)) + (
        a1 * (a1 * g11 + 2.0 * a0 * g01) + a0 * a0 * g00
    )
    h21 = jnp.sqrt(jnp.maximum(norm, 0.0) + EPSILON)
    radius = jnp.sqrt(h00 * h00 + h10 * h10)
    cos0, sin0 = h00 / radius, h10 / radius
    top = cos0 * h01 + sin0 * h11
    low = cos0 * h11 - sin0 * h01
    length = jnp.sqrt(low * low + h21 * h21)
    y1 = (low / length) * (-sin0 * beta) / length
    y0 = (cos0 * beta - top * y1) / radius
    return y0 / beta + y1 * c0, y1 * c1


def on_device(
    n_gx,
    n_yz,
    source,
    mass,
    coupling,
    flux,
    first,
    final,
    middle,
    adjacent,
    plane,
    band,
    small,
    proprietor,
    outq,
    incm,
    incq,
    cmts,
):
    del proprietor
    tables = [jnp.asarray(t) for t in gll_tables()]
    wide, slots = 8 * n_yz, CAP * n_yz
    arguments = (
        source, mass, coupling, flux, first, final, middle, adjacent, plane, band,
        small, outq, incm, incq, cmts, *tables,
    )
    hbm = pl.BlockSpec(memory_space=pltpu.HBM)
    return pl.pallas_call(
        functools.partial(kernel, n_gx, n_yz, cmts.shape[1]),
        out_shape=jax.ShapeDtypeStruct(source.shape, F32),
        in_specs=[hbm] * len(arguments),
        out_specs=hbm,
        scratch_shapes=[
            pltpu.VMEM(source.shape, F32),
            *[pltpu.VMEM(a.shape, a.dtype) for a in arguments],
            pltpu.SemaphoreType.DMA((len(arguments),)),
            pltpu.VMEM((2, 2, wide // 2, 128), F32),
            pltpu.VMEM((2, wide, 128), F32),
            pltpu.VMEM((2, 4, HALO, 128), F32),
            pltpu.VMEM((2, 4, HALO, 128), F32),
            pltpu.VMEM((1, 128), F32),
            pltpu.VMEM((n_gx, 1, 128), F32),
            pltpu.VMEM((1, 128), F32),
            pltpu.VMEM((n_yz, 1, 128), F32),
            pltpu.VMEM((768, 4 * wide // 2 + 128), BF16),
            pltpu.VMEM((768, 768), BF16),
            pltpu.VMEM((2 * slots + 128, 768), BF16),
            pltpu.VMEM((480, 640), BF16),
            pltpu.VMEM((2, 320, 480), BF16),
            pltpu.VMEM((2 * FACE, 768), BF16),
            pltpu.VMEM((2, 320, 128), F32),
            pltpu.SemaphoreType.DMA((3, 2)),
            pltpu.SemaphoreType.DMA((3, 2)),
            pltpu.SemaphoreType.DMA((2,)),
        ],
        compiler_params=pltpu.CompilerParams(
            collective_id=0, has_side_effects=True, vmem_limit_bytes=63 * 1024 * 1024
        ),
    )(*arguments)


def solution(mesh):
    n_gx, n_yz = mesh.shape["gx"], mesh.shape["yz"]
    both = ("gx", "yz")
    field, lists = P(None, both), P(both, None)
    return jax.shard_map(
        functools.partial(on_device, n_gx, n_yz),
        mesh=mesh,
        in_specs=(
            field, field, field, field, P(), P(), field, field,
            P(both, None, None), P(both, None, None),
            lists, lists, lists, lists, lists, lists,
        ),
        out_specs=field,
        check_vma=False,
    )
```
